512 devices in a mesh: grp: 32 (over z, core), tp: 16 (over x, y).
Axes of the slice: x: 4, y: 4, z: 16, core: 2. Of those that a mesh axis runs over, the one named last changes fastest.
Arguments:
- query_nope: bfloat16 [8192, 8192], P('grp', 'tp'), may hold values from -6 to 6
- query_rope: bfloat16 [8192, 4096], P('grp', 'tp'), may hold values from -24 to 24
- latent_cache: bfloat16 [65536, 576], P('grp'), may hold values from -6 to 6
- new_latent: bfloat16 [64, 128, 576], P('grp', 'tp'), may hold values from -6 to 6
- prefix_length: int32 [32], P('grp'), may hold values from 2 to 2048, as said below
- latent_up: bfloat16 [512, 16384], P(None, 'tp'), may hold values from -0.5 to 0.5
- out_proj: bfloat16 [8192, 4096], P('tp', 'grp'), may hold values from -0.25 to 0.25
- owners: int32 [64], replicated, may hold values from 0 to 31, as said below
- slot_index: int32 [64], replicated, may hold values from 0 to 3, as said below
Outputs:
- mixed: bfloat16 [8192, 4096], P(('grp', 'tp'))
- decode_cache: bfloat16 [128, 128, 576], P('grp', 'tp')
The draws below stay inside these ranges and needn't reach their ends.
Inputs may be any that keep to these rules, and one draw needn't show every extreme that they name: `prefix_length`: some group uses all 2048 cached positions. Each owner receives at most 4 blocks, and some owner receives exactly 4; the 2 blocks of one group have different owners. `slot_index`: blocks of one owner have different slots.
All inputs are finite; a program needn't handle non-finite values.
Results may differ from the reference program's by a relative error of at most 0.018.
Values may be sent and summed in bfloat16 or wider, within the bound.
A program may use at most 64 MiB of HBM per device.

```python
import jax
import jax.numpy as jnp
from jax import lax

D = 4096
HEADS = 64
NOPE = 128
ROPE = 64
VDIM = 128
KVR = 512
KVW = 576
SPAN = 256
PREFIX = 2048
BLOCK = 128
BPG = 2
SLOTS = 4
GROUPS = 32
NBLK = 64
TOKENS = 8192
N_TP = 16


def block_tokens(key):
    first, second, third, fourth = jax.random.split(jax.random.fold_in(key, 200), 4)
    count = GROUPS * SLOTS
    priority = jax.random.permutation(first, count)
    favored = jax.random.randint(second, (), 0, GROUPS)
    tokens_all = jnp.arange(count, dtype=jnp.int32)
    priority = priority - jnp.where(tokens_all // SLOTS == favored, count, 0)
    ordered = jnp.argsort(priority, stable=True)
    chosen = jnp.sort(ordered[:NBLK])
    place = jnp.arange(NBLK, dtype=jnp.int32)
    group_labels = jax.random.permutation(third, GROUPS)
    owner_labels = jax.random.permutation(fourth, GROUPS)
    first_owner = chosen[0] // SLOTS
    owner_labels = (owner_labels - owner_labels[first_owner] + group_labels[0] + GROUPS // 2) % GROUPS
    target = group_labels[place % GROUPS] * BPG + place // GROUPS
    owner_of = owner_labels[chosen // SLOTS].astype(jnp.int32)
    slot_of = (chosen % SLOTS).astype(jnp.int32)
    owner_out = jnp.zeros((NBLK,), jnp.int32).at[target].set(owner_of)
    slot_out = jnp.zeros((NBLK,), jnp.int32).at[target].set(slot_of)
    return (owner_out, slot_out)


def draw_query_nope(key, part):
    key = jax.random.fold_in(key, 1)
    values = jnp.clip(jax.random.normal(key, (TOKENS, HEADS * NOPE), jnp.float32), -6.0, 6.0)
    return values.astype(jnp.bfloat16)


def draw_query_rope(key, part):
    key = jax.random.fold_in(key, 2)
    values = jnp.clip(jax.random.normal(key, (TOKENS, HEADS * ROPE), jnp.float32), -6.0, 6.0)
    return values.astype(jnp.bfloat16)


def draw_latent_cache(key, part):
    key = jax.random.fold_in(key, 3)
    values = jnp.clip(jax.random.normal(key, (GROUPS * PREFIX, KVW), jnp.float32), -6.0, 6.0)
    return values.astype(jnp.bfloat16)


def draw_prefix_length(key, part):
    key = jax.random.fold_in(key, 5)
    lengths = jax.random.randint(key, (GROUPS,), 2, PREFIX + 1)
    picked = jax.random.randint(jax.random.fold_in(key, 6), (), 0, GROUPS)
    return jnp.where(jnp.arange(GROUPS) == picked, PREFIX, lengths).astype(jnp.int32)


def draw_owners(key, part):
    return block_tokens(key)[0]


def draw_slot_index(key, part):
    return block_tokens(key)[1]


def shard_levels(own_key, extent, cuts, smallest, high):
    loudness, own = 1.0, jax.random.fold_in(own_key, 6)
    for position, blocks in cuts:
        heights = jnp.exp(jax.random.uniform(jax.random.fold_in(own, position), (blocks,), jnp.float32, smallest / len(cuts), high / len(cuts)))
        loudness = loudness * jnp.repeat(heights, extent[position] // blocks).reshape([-1 if axis == position else 1 for axis in range(len(extent))])
    return loudness


def noise(key, shape, width, most, pieces=(), kind=jnp.bfloat16):
    values = width * jax.random.normal(key, shape, jnp.float32)
    if pieces:
        values = values * shard_levels(key, shape, pieces, -0.22, 0.18)
    return jnp.clip(values, -most, most).astype(kind)


def setup_inputs(seed: int = 0) -> dict:
    key_of = jax.random.split(jax.random.key(seed), 10)
    return {
        "query_nope": draw_query_nope(jax.random.fold_in(key_of[9], 71), 0),
        "query_rope": draw_query_rope(jax.random.fold_in(key_of[9], 71), 0),
        "latent_cache": draw_latent_cache(jax.random.fold_in(key_of[9], 71), 0),
        "new_latent": noise(key_of[3], (NBLK, BLOCK, KVW), 1.0, 6.0, ((0, 32), (1, 16))),
        "prefix_length": draw_prefix_length(jax.random.fold_in(key_of[9], 71), 0),
        "latent_up": noise(key_of[5], (KVR, HEADS * (NOPE + VDIM)), NOPE ** -0.5, 0.5, ((1, 16),)),
        "out_proj": noise(key_of[6], (HEADS * VDIM, D), (HEADS * 8) ** -0.5, 0.25, ((0, 16), (1, 32))),
        "owners": draw_owners(jax.random.fold_in(key_of[9], 71), 0),
        "slot_index": draw_slot_index(jax.random.fold_in(key_of[9], 71), 0),
    }


def group_attention(query_nope, query_rope, key_rows, length, latent_up):
    span = query_nope.shape[0]
    total = key_rows.shape[0]
    prefix = total - span
    score_scale = (NOPE + ROPE) ** -0.5
    row_ids = jnp.arange(span, dtype=jnp.int32)[:, None]
    col_ids = jnp.arange(total, dtype=jnp.int32)[None, :]
    visible = jnp.where(col_ids < prefix, col_ids < length, col_ids - prefix <= row_ids)
    nope_heads = query_nope.reshape(span, HEADS, NOPE).transpose(1, 0, 2)
    rope_heads = query_rope.reshape(span, HEADS, ROPE).transpose(1, 0, 2)
    up_heads = latent_up.reshape(KVR, HEADS, NOPE + VDIM).transpose(1, 0, 2)

    def one_head(items):
        nope_part, rope_part, up_part = items
        absorbed = jnp.dot(nope_part, up_part[:, :NOPE].T, preferred_element_type=jnp.float32).astype(jnp.bfloat16)
        queries = jnp.concatenate([absorbed, rope_part], axis=1)
        scores = jnp.dot(queries, key_rows.T, preferred_element_type=jnp.float32) * score_scale
        scores = jnp.where(visible, scores, -jnp.inf)
        highest = jnp.max(scores, axis=1, keepdims=True)
        expo = jnp.exp(scores - highest)
        soft_weights = (expo / jnp.sum(expo, axis=1, keepdims=True)).astype(jnp.bfloat16)
        latent_out = jnp.dot(soft_weights, key_rows[:, :KVR], preferred_element_type=jnp.float32).astype(jnp.bfloat16)
        return jnp.dot(latent_out, up_part[:, NOPE:], preferred_element_type=jnp.float32).astype(jnp.bfloat16)

    outputs = lax.map(one_head, (nope_heads, rope_heads, up_heads))
    return outputs.transpose(1, 0, 2).reshape(span, HEADS * VDIM)


def reference(query_nope, query_rope, latent_cache, new_latent, prefix_length, latent_up, out_proj, owners, slot_index):
    fresh = new_latent.reshape(GROUPS, SPAN, KVW)
    cached = latent_cache.reshape(GROUPS, PREFIX, KVW)

    def per_group(items):
        nope_part, rope_part, cache_part, fresh_part, length = items
        key_rows = jnp.concatenate([cache_part, fresh_part], axis=0)
        return group_attention(nope_part, rope_part, key_rows, length, latent_up)

    outputs = lax.map(per_group, (query_nope.reshape(GROUPS, SPAN, HEADS * NOPE), query_rope.reshape(GROUPS, SPAN, HEADS * ROPE), cached, fresh, prefix_length))
    attended = outputs.reshape(GROUPS * SPAN, HEADS * VDIM)
    rows_rank = HEADS * VDIM // N_TP
    summed = jnp.zeros((GROUPS * SPAN, D), jnp.float32)
    for rank in range(N_TP):
        partial_value = jnp.dot(attended[:, rank * rows_rank:(rank + 1) * rows_rank], out_proj[rank * rows_rank:(rank + 1) * rows_rank], preferred_element_type=jnp.float32)
        rounded = lax.optimization_barrier(partial_value.astype(jnp.bfloat16))
        summed = summed + rounded.astype(jnp.float32)
    mixed = summed.astype(jnp.bfloat16)
    targets = jnp.arange(GROUPS * SLOTS, dtype=jnp.int32)
    selector = ((owners[None, :] == (targets // SLOTS)[:, None]) & (slot_index[None, :] == (targets % SLOTS)[:, None])).astype(jnp.bfloat16)
    picked = jnp.dot(selector, new_latent.reshape(NBLK, BLOCK * KVW), preferred_element_type=jnp.float32)
    decode_cache = picked.astype(jnp.bfloat16).reshape(GROUPS * SLOTS, BLOCK, KVW)
    return (mixed, decode_cache)
```

```python
import jax
import jax.numpy as jnp
from jax import lax
from jax.experimental import pallas as pl
from jax.experimental.pallas import tpu as pltpu
from jax.sharding import PartitionSpec as P

NOPE = 128
ROPE = 64
VDIM = 128
KVR = 512
KVW = 576
SLOTS = 4
SPAN = 256
PREFIX = 2048
KEYS = PREFIX + SPAN
HEADS_DEV = 4
GRP = 32
Z = 16
W_ROWS = 512
NL_ROWS = 80
BLK_ROWS = W_ROWS + NL_ROWS
CHUNKS = ((0, 304), (304, 288))
LAST = 15
MESH = pl.DeviceIdType.MESH
F32 = jnp.float32
BF16 = jnp.bfloat16


def kernel(
    len_ref, own_ref, slot_ref, qn_hbm, qr_hbm, cache_hbm, nl_hbm, up_hbm, w_hbm,
    mixed_ref, dec_ref,
    qn, qr, cache, up, nl, fresh, kv, ropes, ring, att, part, p1, mid, p2, res, res_in, dec, dec_in,
    in_sem, ring_send, ring_recv, nlx_send, nlx_recv, nly_send, nly_recv, att_sem,
    p1_send, p1_recv, p2_send, p2_recv, res_send, res_recv, dec_sem,
):
    g = lax.axis_index("grp")
    t = lax.axis_index("tp")
    z, core = g // 2, lax.rem(g, 2)
    x, y = t // 4, lax.rem(t, 4)
    up_z = {"grp": lax.rem(g + 2, GRP)}
    down_z = {"grp": lax.rem(g + GRP - 2, GRP)}
    sibling = {"grp": g + 1 - 2 * core}
    xs = [lax.rem(x + d, 4) for d in (1, 2, 3)]
    ys = [lax.rem(y + d, 4) for d in (1, 2, 3)]
    x_peers = [{"tp": xx * 4 + y} for xx in xs]
    y_peers = [{"tp": x * 4 + yy} for yy in ys]

    loads = [
        pltpu.make_async_copy(w_hbm, ring.at[0, pl.ds(0, W_ROWS)], in_sem.at[0]),
        pltpu.make_async_copy(nl_hbm, nl, in_sem.at[1]),
        pltpu.make_async_copy(up_hbm, up, in_sem.at[2]),
        pltpu.make_async_copy(cache_hbm, cache, in_sem.at[3]),
        pltpu.make_async_copy(qn_hbm, qn, in_sem.at[4]),
        pltpu.make_async_copy(qr_hbm, qr, in_sem.at[5]),
    ]
    for load in loads:
        load.start()
    barrier = pltpu.get_barrier_semaphore()
    partners = [up_z, down_z, sibling] + x_peers + y_peers
    for who in partners:
        pl.semaphore_signal(barrier, inc=1, device_id=who, device_id_type=MESH)
    loads[1].wait()
    rows = nl[...]
    tiles = [rows[:, k * 128 : (k + 1) * 128] for k in range(4)]
    tiles.append(jnp.concatenate([rows[:, KVR:], jnp.zeros((16, 64), BF16)], axis=1))
    packed = jnp.concatenate(tiles, axis=0)
    ring[0, pl.ds(W_ROWS, NL_ROWS), :] = packed
    fresh[x, y] = packed
    loads[0].wait()
    pl.semaphore_wait(barrier, len(partners))

    def remote(src, dst, send, recv, who):
        return pltpu.make_async_remote_copy(
            src_ref=src, dst_ref=dst, send_sem=send, recv_sem=recv, device_id=who, device_id_type=MESH
        )

    def hop(src, dst, k, who):
        at, n = CHUNKS[k]
        return remote(
            ring.at[src, pl.ds(at, n)], ring.at[dst, pl.ds(at, n)], ring_send.at[dst, k], ring_recv.at[dst, k], who
        )

    def send_first():
        for k in range(len(CHUNKS)):
            hop(0, 1, k, up_z).start()
            hop(0, 8, k, down_z).start()

    def service(s):
        for k in range(len(CHUNKS)):
            hop(s - 1, s, k, up_z).wait_recv()
            if s < 7:
                hop(s, s + 1, k, up_z).start()
            elif k < len(CHUNKS) // 2:
                hop(s, LAST, k, up_z).start()
            hop(s + 6, s + 7, k, down_z).wait_recv()
            if s < 7:
                hop(s + 7, s + 8, k, down_z).start()
            elif k >= len(CHUNKS) // 2:
                hop(s + 7, LAST, k, down_z).start()

    def service_last():
        for k in range(len(CHUNKS)):
            hop(7, LAST, k, up_z).wait_recv()

    def nlx(i):
        return remote(fresh.at[x, y], fresh.at[x, y], nlx_send.at[i], nlx_recv.at[i], x_peers[i])

    def nlx_from(i):
        src = lax.rem(x + 3 - i, 4)
        return remote(fresh.at[src, y], fresh.at[src, y], nlx_send.at[i], nlx_recv.at[i], x_peers[i])

    def nly(i):
        return remote(fresh.at[:, y], fresh.at[:, y], nly_send.at[i], nly_recv.at[i], y_peers[i])

    def nly_from(i):
        src = lax.rem(y + 3 - i, 4)
        return remote(fresh.at[:, src], fresh.at[:, src], nly_send.at[i], nly_recv.at[i], y_peers[i])

    for i in range(3):
        nlx(i).start()
    send_first()

    def project_keys(lat, rope, at, n):
        kv[pl.ds(at, n), :] = jnp.dot(lat, up[...], preferred_element_type=F32).astype(BF16)
        zero = jnp.zeros((n, 64), BF16)
        ropes[0, pl.ds(at, n), :] = jnp.concatenate([rope, zero], axis=1)
        ropes[1, pl.ds(at, n), :] = jnp.concatenate([zero, rope], axis=1)

    for i in (2, 3):
        loads[i].wait()

    def prefix_keys(i, _):
        at = pl.multiple_of(i * 256, 256)
        project_keys(cache[pl.ds(at, 256), :KVR], cache[pl.ds(at, 256), KVR:], at, 256)
        return _

    lax.fori_loop(0, 4, prefix_keys, 0)
    for i in range(3):
        nlx_from(i).wait_recv()
    for i in range(3):
        nly(i).start()
    lax.fori_loop(4, 8, prefix_keys, 0)
    service(1)
    for i in range(3):
        nly_from(i).wait_recv()
    new = fresh[...].reshape(16, 5, 16, 128)
    new = [new[:, k].reshape(SPAN, 128) for k in range(5)]
    project_keys(jnp.concatenate(new[:4], axis=1), new[4][:, :64], PREFIX, SPAN)

    for i in (4, 5):
        loads[i].wait()
    to_bits = (NOPE + ROPE) ** -0.5 * 1.4426950408889634
    col = lax.broadcasted_iota(jnp.int32, (1, PREFIX), 1)
    old_bias = jnp.where(col < len_ref[0], 0.0, -1e30).astype(F32)
    row = lax.broadcasted_iota(jnp.int32, (SPAN, SPAN), 0)
    key = lax.broadcasted_iota(jnp.int32, (SPAN, SPAN), 1)
    token = ((key // 8) % 2) * 128 + (key // 16) * 8 + key % 8
    new_bias = jnp.where(token <= row, 0.0, -1e30).astype(F32)

    def head(h):
        k = jnp.concatenate([kv[:, h * 256 : h * 256 + NOPE], ropes[h % 2]], axis=1)
        pair = h // 2
        q = jnp.concatenate([qn[:, h * 128 : (h + 1) * 128], qr[:, pair * 128 : (pair + 1) * 128]], axis=1)
        s = lax.dot_general(q, k, (((1,), (1,)), ((), ())), preferred_element_type=F32)
        s = jnp.concatenate([s[:, :PREFIX] + old_bias, s[:, PREFIX:] + new_bias], axis=1)
        highest = jnp.max(s, axis=1, keepdims=True)
        e = jnp.exp2((s - highest) * to_bits)
        total = jnp.sum(e, axis=1, keepdims=True)
        v = kv[:, h * 256 + NOPE : (h + 1) * 256]
        o = jnp.dot(e.astype(BF16), v, preferred_element_type=F32)
        att[0, :, h * 128 : (h + 1) * 128] = (o / total).astype(BF16)

    head(0)
    service(2)
    head(1)
    head(2)
    service(3)
    head(3)
    swap = remote(att.at[0], att.at[1], att_sem.at[0], att_sem.at[1], sibling)
    swap.start()
    swap.wait_recv()

    def plane_of(b):
        if b < 8:
            return lax.rem(z + Z - b, Z)
        if b == LAST:
            return lax.rem(z + 8, Z)
        return lax.rem(z + b - 7, Z)

    def out_first(b, i):
        src = part.at[b, :, xs[i]] if b < 8 else part.at[b, :, :, ys[i]]
        who = x_peers[i] if b < 8 else y_peers[i]
        return remote(src, p1.at[b, i], p1_send.at[b, i], p1_recv.at[b, i], who)

    def out_second(b, i):
        src = mid.at[b, :, ys[i]] if b < 8 else mid.at[b, :, xs[i]]
        who = y_peers[i] if b < 8 else x_peers[i]
        return remote(src, p2.at[b, i], p2_send.at[b, i], p2_recv.at[b, i], who)

    def out_res(b):
        return remote(res.at[b], res_in.at[b], res_send.at[b], res_recv.at[b], sibling)

    def project(blocks):
        w = jnp.concatenate([ring[b, pl.ds(0, W_ROWS), :] for b in blocks], axis=1)
        a = att[...].reshape(2 * SPAN, W_ROWS)
        o = jnp.dot(a, w, preferred_element_type=F32).astype(BF16)
        for n, b in enumerate(blocks):
            part[b] = o[:, n * 128 : (n + 1) * 128].reshape(2, 4, 4, 16, 128)
        for i in range(3):
            for b in blocks:
                out_first(b, i).start()

    def first_sum(blocks):
        for b in blocks:
            for i in range(3):
                out_first(b, i).wait_recv()
            own = part[b, :, x] if b < 8 else part[b, :, :, y]
            total = own.astype(F32)
            for i in range(3):
                total += p1[b, i].astype(F32)
            mid[b] = total.astype(BF16)
            for i in range(3):
                out_second(b, i).start()

    def second_sum(blocks):
        for b in blocks:
            for i in range(3):
                out_second(b, i).wait_recv()
            own = mid[b, :, y] if b < 8 else mid[b, :, x]
            total = own.astype(F32)
            for i in range(3):
                total += p2[b, i].astype(F32)
            total = total.astype(BF16)
            res[b] = total[1]
            out_res(b).start()
            at = pl.multiple_of((2 * plane_of(b) + core) * 128, 128)
            mixed_ref[:, pl.ds(at, 128)] = total[0]

    def collect(blocks):
        for b in blocks:
            out_res(b).wait_recv()
            at = pl.multiple_of((2 * plane_of(b) + 1 - core) * 128, 128)
            mixed_ref[:, pl.ds(at, 128)] = res_in[b]

    steps = [(0,)] + [(s, s + 7) for s in range(1, 8)] + [(LAST,)]
    done = 3
    for s in range(9):
        if s > done:
            if s < 8:
                service(s)
            else:
                service_last()
        project(steps[s])
        if s >= 1:
            first_sum(steps[s - 1])
        if s >= 2:
            second_sum(steps[s - 2])
    first_sum(steps[8])
    second_sum(steps[7])

    def pick(owner, s):
        def look(b, carry):
            slot, half = carry
            plane, i = b // 2, lax.rem(b, 2)
            block = 2 * (2 * plane + core) + i
            hit = jnp.logical_and(own_ref[block] == owner, slot_ref[block] == s)
            away = lax.rem(z - plane + Z, Z)
            place = jnp.where(away < 8, away, jnp.where(away == 8, LAST, 23 - away))
            return jnp.where(hit, place, slot), jnp.where(hit, i, half)

        slot, half = lax.fori_loop(0, 2 * Z, look, (jnp.int32(-1), jnp.int32(0)))
        got = ring[jnp.maximum(slot, 0), pl.ds(W_ROWS, NL_ROWS), :].reshape(5, 16, 128).astype(F32)
        got = jnp.where(half == 0, got[:, :8], got[:, 8:])
        got = jnp.where(slot >= 0, got, 0.0)
        return jnp.concatenate([got[k] for k in range(5)], axis=1)

    for s in range(0, SLOTS, 2):
        both = jnp.concatenate([pick(g + 1 - 2 * core, s), pick(g + 1 - 2 * core, s + 1)], axis=0)
        dec[s // 2] = both.astype(BF16)
    swap_dec = remote(dec, dec_in, dec_sem.at[0], dec_sem.at[1], sibling)
    swap_dec.start()
    mine = [pick(g, s) for s in range(SLOTS)]
    swap_dec.wait_recv()
    for s in range(SLOTS):
        other = dec_in[s // 2].astype(F32)[(s % 2) * 8 : (s % 2) * 8 + 8]
        dec_ref[s] = (mine[s] + other)[:, :KVW].astype(BF16)

    second_sum(steps[8])
    for blocks in steps:
        collect(blocks)

    for k in range(len(CHUNKS)):
        for s in range(7):
            hop(s, s + 1, k, up_z).wait_send()
            hop(s + 7 if s else 0, s + 8, k, down_z).wait_send()
        hop(7, LAST, k, up_z).wait_send()
    for i in range(3):
        nlx(i).wait_send()
        nly(i).wait_send()
    swap.wait_send()
    swap_dec.wait_send()
    for b in range(16):
        for i in range(3):
            out_first(b, i).wait_send()
            out_second(b, i).wait_send()
        out_res(b).wait_send()


def body(query_nope, query_rope, latent_cache, new_latent, prefix_length, latent_up, out_proj, owners, slot_index):
    nl = new_latent.reshape(16, KVW)
    smem = pl.BlockSpec(memory_space=pltpu.SMEM)
    hbm = pl.BlockSpec(memory_space=pl.ANY)
    vmem = pl.BlockSpec(memory_space=pltpu.VMEM)
    dma = pltpu.SemaphoreType.DMA
    nk = len(CHUNKS)
    return pl.pallas_call(
        kernel,
        out_shape=(
            jax.ShapeDtypeStruct((16, 4096), BF16),
            jax.ShapeDtypeStruct((SLOTS, 8, KVW), BF16),
        ),
        in_specs=[smem] * 3 + [hbm] * 6,
        out_specs=(vmem, vmem),
        scratch_shapes=[
            pltpu.VMEM((SPAN, 512), BF16),
            pltpu.VMEM((SPAN, 256), BF16),
            pltpu.VMEM((PREFIX, KVW), BF16),
            pltpu.VMEM((KVR, 1024), BF16),
            pltpu.VMEM((16, KVW), BF16),
            pltpu.VMEM((4, 4, NL_ROWS, 128), BF16),
            pltpu.VMEM((KEYS, 1024), BF16),
            pltpu.VMEM((2, KEYS, 128), BF16),
            pltpu.VMEM((16, BLK_ROWS, 128), BF16),
            pltpu.VMEM((2, SPAN, 512), BF16),
            pltpu.VMEM((16, 2, 4, 4, 16, 128), BF16),
            pltpu.VMEM((16, 3, 2, 4, 16, 128), BF16),
            pltpu.VMEM((16, 2, 4, 16, 128), BF16),
            pltpu.VMEM((16, 3, 2, 16, 128), BF16),
            pltpu.VMEM((16, 16, 128), BF16),
            pltpu.VMEM((16, 16, 128), BF16),
            pltpu.VMEM((2, 16, 640), BF16),
            pltpu.VMEM((2, 16, 640), BF16),
            dma((6,)),
            dma((16, nk)),
            dma((16, nk)),
            dma((3,)),
            dma((3,)),
            dma((3,)),
            dma((3,)),
            dma((2,)),
            dma((16, 3)),
            dma((16, 3)),
            dma((16, 3)),
            dma((16, 3)),
            dma((16,)),
            dma((16,)),
            dma((2,)),
        ],
        compiler_params=pltpu.CompilerParams(
            collective_id=0, has_side_effects=True, vmem_limit_bytes=56 * 1024 * 1024
        ),
        cost_estimate=pl.CostEstimate(flops=5_000_000_000, bytes_accessed=6_000_000, transcendentals=2_400_000),
    )(prefix_length, owners, slot_index, query_nope, query_rope, latent_cache, nl, latent_up, out_proj)


def solution(mesh):
    placed = (
        P("grp", "tp"),
        P("grp", "tp"),
        P("grp", None),
        P("grp", "tp", None),
        P("grp"),
        P(None, "tp"),
        P("tp", "grp"),
        P(),
        P(),
    )
    return jax.shard_map(
        body,
        mesh=mesh,
        in_specs=placed,
        out_specs=(P(("grp", "tp"), None), P("grp", "tp", None)),
        check_vma=False,
    )
```

```python
import jax
import jax.numpy as jnp
from jax import lax
from jax.experimental import pallas as pl
from jax.experimental.pallas import tpu as pltpu
from jax.sharding import PartitionSpec as P

NOPE = 128
ROPE = 64
VDIM = 128
KVR = 512
KVW = 576
SLOTS = 4
SPAN = 256
PREFIX = 2048
KEYS = PREFIX + SPAN
HEADS_DEV = 4
GRP = 32
Z = 16
W_ROWS = 512
NL_ROWS = 80
BLK_ROWS = W_ROWS + NL_ROWS
CHUNKS = ((0, 304), (304, 288))
DIRECT = (7, 14, 15)
LAST = 15
MESH = pl.DeviceIdType.MESH
F32 = jnp.float32
BF16 = jnp.bfloat16


def kernel(
    len_ref, own_ref, slot_ref, qn_hbm, qr_hbm, cache_hbm, nl_hbm, up_hbm, w_hbm,
    mixed_ref, dec_ref,
    qn, qr, cache, up, nl, fresh, up_t, kv, ropes, ring, att, part, p1, mid, p2, direct, res, res_in, dec, dec_in,
    in_sem, ring_send, ring_recv, nl_sem, att_sem,
    p1_send, p1_recv, p2_send, p2_recv, direct_send, direct_recv, res_send, res_recv, dec_sem,
):
    g = lax.axis_index("grp")
    t = lax.axis_index("tp")
    z, core = g // 2, lax.rem(g, 2)
    x, y = t // 4, lax.rem(t, 4)
    up_z = {"grp": lax.rem(g + 2, GRP)}
    down_z = {"grp": lax.rem(g + GRP - 2, GRP)}
    sibling = {"grp": g + 1 - 2 * core}
    xs = [lax.rem(x + d, 4) for d in (1, 2, 3)]
    ys = [lax.rem(y + d, 4) for d in (1, 2, 3)]
    x_peers = [{"tp": xx * 4 + y} for xx in xs]
    y_peers = [{"tp": x * 4 + yy} for yy in ys]

    loads = [
        pltpu.make_async_copy(w_hbm, ring.at[0, pl.ds(0, W_ROWS)], in_sem.at[0]),
        pltpu.make_async_copy(nl_hbm, nl, in_sem.at[1]),
        pltpu.make_async_copy(up_hbm, up, in_sem.at[2]),
        pltpu.make_async_copy(cache_hbm, cache, in_sem.at[3]),
        pltpu.make_async_copy(qn_hbm, qn, in_sem.at[4]),
        pltpu.make_async_copy(qr_hbm, qr, in_sem.at[5]),
    ]
    for load in loads:
        load.start()
    barrier = pltpu.get_barrier_semaphore()
    plane = [(dx, dy) for dx in range(4) for dy in range(4)][1:]
    plane_xy = [(lax.rem(x + dx, 4), lax.rem(y + dy, 4)) for dx, dy in plane]
    plane_peers = [{"tp": xx * 4 + yy} for xx, yy in plane_xy]
    partners = [up_z, down_z, sibling] + plane_peers
    for who in partners:
        pl.semaphore_signal(barrier, inc=1, device_id=who, device_id_type=MESH)
    loads[1].wait()
    rows = nl[...]
    tiles = [rows[:, k * 128 : (k + 1) * 128] for k in range(4)]
    tiles.append(jnp.concatenate([rows[:, KVR:], jnp.zeros((16, 64), BF16)], axis=1))
    packed = jnp.concatenate(tiles, axis=0)
    ring[0, pl.ds(W_ROWS, NL_ROWS), :] = packed
    fresh[t] = packed
    loads[0].wait()
    pl.semaphore_wait(barrier, len(partners))

    def remote(src, dst, send, recv, who):
        return pltpu.make_async_remote_copy(
            src_ref=src, dst_ref=dst, send_sem=send, recv_sem=recv, device_id=who, device_id_type=MESH
        )

    def hop(src, dst, k, who):
        at, n = CHUNKS[k]
        return remote(
            ring.at[src, pl.ds(at, n)], ring.at[dst, pl.ds(at, n)], ring_send.at[dst, k], ring_recv.at[dst, k], who
        )

    def send_first():
        for k in range(len(CHUNKS)):
            hop(0, 1, k, up_z).start()
            hop(0, 8, k, down_z).start()

    def service(s, k):
        hop(s - 1, s, k, up_z).wait_recv()
        if s < 7:
            hop(s, s + 1, k, up_z).start()
        elif k == 0:
            hop(s, LAST, k, up_z).start()
        hop(s + 6, s + 7, k, down_z).wait_recv()
        if s < 7:
            hop(s + 7, s + 8, k, down_z).start()
        elif k == 1:
            hop(s + 7, LAST, k, down_z).start()

    def service_last():
        for k in range(len(CHUNKS)):
            hop(7, LAST, k, up_z).wait_recv()

    def new_rows(i):
        return remote(fresh.at[t], fresh.at[t], nl_sem.at[0], nl_sem.at[1], plane_peers[i])

    others = fresh.at[pl.ds(0, 15)]
    all_new_rows = remote(others, others, nl_sem.at[0], nl_sem.at[1], plane_peers[0])

    send_first()
    for i in range(15):
        new_rows(i).start()

    def look(b, codes):
        plane, i = b // 2, lax.rem(b, 2)
        block = 2 * (2 * plane + core) + i
        owner, place = own_ref[block], slot_ref[block]
        away = lax.rem(z - plane + Z, Z)
        code = 2 * jnp.where(away < 8, away, jnp.where(away == 8, LAST, 23 - away)) + i
        wanted = [(who, s) for who in (g, g + 1 - 2 * core) for s in range(SLOTS)]
        return tuple(
            jnp.where(jnp.logical_and(owner == who, place == s), code, old)
            for (who, s), old in zip(wanted, codes, strict=True)
        )

    codes = lax.fori_loop(0, 2 * Z, look, (jnp.int32(-1),) * (2 * SLOTS))

    def rope_rows(rope, at, n):
        zero = jnp.zeros((64, n), BF16)
        ropes[0, :, pl.ds(at, n)] = jnp.concatenate([rope, zero], axis=0)
        ropes[1, :, pl.ds(at, n)] = jnp.concatenate([zero, rope], axis=0)

    for i in (2, 3):
        loads[i].wait()

    up_t[...] = up[...].T

    def prefix_keys(i, _):
        at = pl.multiple_of(i * 256, 256)
        kv[:, pl.ds(at, 256)] = jnp.dot(
            up_t[...], cache[pl.ds(0, KVR), pl.ds(at, 256)], preferred_element_type=F32
        ).astype(BF16)
        rope_rows(cache[pl.ds(KVR, ROPE), pl.ds(at, 256)], at, 256)
        return _

    lax.fori_loop(0, 8, prefix_keys, 0)
    service(1, 0)
    all_new_rows.wait_recv()
    new = fresh[...].reshape(16, 5, 16, 128)
    new = [new[:, k].reshape(SPAN, 128) for k in range(5)]
    kv[:, pl.ds(PREFIX, SPAN)] = lax.dot_general(
        up_t[...], jnp.concatenate(new[:4], axis=1), (((1,), (1,)), ((), ())), preferred_element_type=F32
    ).astype(BF16)
    rope_rows(new[4].T[:ROPE], PREFIX, SPAN)

    service(1, 1)
    for i in (4, 5):
        loads[i].wait()
    to_bits = (NOPE + ROPE) ** -0.5 * 1.4426950408889634
    col = lax.broadcasted_iota(jnp.int32, (1, PREFIX), 1)
    old_bias = jnp.where(col < len_ref[0], 0.0, -1e30).astype(F32)
    row = lax.broadcasted_iota(jnp.int32, (SPAN, SPAN), 0)
    key = lax.broadcasted_iota(jnp.int32, (SPAN, SPAN), 1)
    token = ((key // 8) % 2) * 128 + (key // 16) * 8 + key % 8
    new_bias = jnp.where(token <= row, 0.0, -1e30).astype(F32)

    def head(h):
        k = jnp.concatenate([kv[h * 256 : h * 256 + NOPE], ropes[h % 2]], axis=0)
        pair = h // 2
        q = jnp.concatenate([qn[:, h * 128 : (h + 1) * 128], qr[:, pair * 128 : (pair + 1) * 128]], axis=1)
        s = jnp.dot(q, k, preferred_element_type=F32)
        s = jnp.concatenate([s[:, :PREFIX] + old_bias, s[:, PREFIX:] + new_bias], axis=1)
        highest = jnp.max(s, axis=1, keepdims=True)
        e = jnp.exp2((s - highest) * to_bits)
        total = jnp.sum(e, axis=1, keepdims=True)
        v = kv[h * 256 + NOPE : (h + 1) * 256]
        o = lax.dot_general(e.astype(BF16), v, (((1,), (1,)), ((), ())), preferred_element_type=F32)
        att[0, :, h * 128 : (h + 1) * 128] = (o / total).astype(BF16)

    head(0)
    service(2, 0)
    head(1)
    service(2, 1)
    head(2)
    service(3, 0)
    head(3)
    swap = remote(att.at[0], att.at[1], att_sem.at[0], att_sem.at[1], sibling)
    swap.start()

    def plane_of(b):
        if b < 8:
            return lax.rem(z + Z - b, Z)
        if b == LAST:
            return lax.rem(z + 8, Z)
        return lax.rem(z + b - 7, Z)

    def out_first(b, i):
        src = part.at[b, :, xs[i]] if b < 8 else part.at[b, :, :, ys[i]]
        who = x_peers[i] if b < 8 else y_peers[i]
        return remote(src, p1.at[b, i], p1_send.at[b, i], p1_recv.at[b, i], who)

    def out_second(b, i):
        src = mid.at[b, :, ys[i]] if b < 8 else mid.at[b, :, xs[i]]
        who = y_peers[i] if b < 8 else x_peers[i]
        return remote(src, p2.at[b, i], p2_send.at[b, i], p2_recv.at[b, i], who)

    def out_direct(b, i):
        n = DIRECT.index(b)
        xx, yy = plane_xy[i]
        return remote(
            part.at[b, :, xx, yy], direct.at[n, i], direct_send.at[n], direct_recv.at[n], plane_peers[i]
        )

    def all_direct(b):
        n = DIRECT.index(b)
        return remote(direct.at[n], direct.at[n], direct_send.at[n], direct_recv.at[n], plane_peers[0])

    def out_res(b):
        return remote(res.at[b], res_in.at[b], res_send.at[b], res_recv.at[b], sibling)

    def project(blocks):
        w = jnp.concatenate([ring[b, pl.ds(0, W_ROWS), :] for b in blocks], axis=1)
        a = att[...].reshape(2 * SPAN, W_ROWS)
        o = jnp.dot(a, w, preferred_element_type=F32).astype(BF16)
        for n, b in enumerate(blocks):
            part[b] = o[:, n * 128 : (n + 1) * 128].reshape(2, 4, 4, 16, 128)
        for i in range(15 if blocks[0] in DIRECT else 3):
            for b in blocks:
                if b in DIRECT:
                    out_direct(b, i).start()
                else:
                    out_first(b, i).start()

    def first_sum(blocks):
        for b in blocks:
            for i in range(3):
                out_first(b, i).wait_recv()
            own = part[b, :, x] if b < 8 else part[b, :, :, y]
            total = own.astype(F32)
            for i in range(3):
                total += p1[b, i].astype(F32)
            mid[b] = total.astype(BF16)
            for i in range(3):
                out_second(b, i).start()

    def deliver(b, total):
        res[b] = total[1]
        out_res(b).start()
        at = pl.multiple_of((2 * plane_of(b) + core) * 128, 128)
        mixed_ref[:, pl.ds(at, 128)] = total[0]

    def direct_sum(blocks):
        for b in blocks:
            all_direct(b).wait_recv()
            total = part[b, :, x, y].astype(F32)
            for i in range(15):
                total += direct[DIRECT.index(b), i].astype(F32)
            deliver(b, total.astype(BF16))

    def second_sum(blocks):
        for b in blocks:
            for i in range(3):
                out_second(b, i).wait_recv()
            own = mid[b, :, y] if b < 8 else mid[b, :, x]
            total = own.astype(F32)
            for i in range(3):
                total += p2[b, i].astype(F32)
            deliver(b, total.astype(BF16))

    def collect(blocks):
        for b in blocks:
            out_res(b).wait_recv()
            at = pl.multiple_of((2 * plane_of(b) + 1 - core) * 128, 128)
            mixed_ref[:, pl.ds(at, 128)] = res_in[b]

    steps = [(0,)] + [(s, s + 7) for s in range(1, 8)] + [(LAST,)]
    service(3, 1)
    swap.wait_recv()
    project(steps[0])
    project(steps[1])
    service(4, 0)
    project(steps[2])
    project(steps[3])
    service(4, 1)
    project(steps[4])
    first_sum(steps[0] + steps[1])
    service(5, 0)
    first_sum(steps[2] + steps[3])
    service(5, 1)
    project(steps[5])
    second_sum(steps[0] + steps[1])
    service(6, 0)
    first_sum(steps[4])
    second_sum(steps[2] + steps[3])
    service(6, 1)
    project(steps[6])
    service(7, 0)
    first_sum(steps[5])
    second_sum(steps[4])
    service(7, 1)
    project(steps[7])
    first_sum(steps[6])
    second_sum(steps[5])
    service_last()
    project(steps[8])
    second_sum(steps[6])
    direct_sum(steps[7])

    def pick(code):
        got = ring[jnp.maximum(code, 0) // 2, pl.ds(W_ROWS, NL_ROWS), :].reshape(5, 16, 128).astype(F32)
        got = jnp.where(lax.rem(jnp.maximum(code, 0), 2) == 0, got[:, :8], got[:, 8:])
        got = jnp.where(code >= 0, got, 0.0)
        return jnp.concatenate([got[k] for k in range(5)], axis=1)

    for s in range(0, SLOTS, 2):
        both = jnp.concatenate([pick(codes[SLOTS + s]), pick(codes[SLOTS + s + 1])], axis=0)
        dec[s // 2] = both.astype(BF16)
    swap_dec = remote(dec, dec_in, dec_sem.at[0], dec_sem.at[1], sibling)
    swap_dec.start()
    mine = [pick(codes[s]) for s in range(SLOTS)]
    swap_dec.wait_recv()
    for s in range(SLOTS):
        other = dec_in[s // 2].astype(F32)[(s % 2) * 8 : (s % 2) * 8 + 8]
        dec_ref[s] = (mine[s] + other)[:, :KVW].astype(BF16)

    direct_sum(steps[8])
    for blocks in steps:
        collect(blocks)

    for k in range(len(CHUNKS)):
        for s in range(7):
            hop(s, s + 1, k, up_z).wait_send()
            hop(s + 7 if s else 0, s + 8, k, down_z).wait_send()
        hop(7, LAST, k, up_z).wait_send()
    all_new_rows.wait_send()
    swap.wait_send()
    swap_dec.wait_send()
    for b in range(16):
        if b in DIRECT:
            all_direct(b).wait_send()
        else:
            for i in range(3):
                out_first(b, i).wait_send()
                out_second(b, i).wait_send()
        out_res(b).wait_send()


def body(query_nope, query_rope, latent_cache, new_latent, prefix_length, latent_up, out_proj, owners, slot_index):
    nl = new_latent.reshape(16, KVW)
    cache = latent_cache.T
    smem = pl.BlockSpec(memory_space=pltpu.SMEM)
    hbm = pl.BlockSpec(memory_space=pl.ANY)
    vmem = pl.BlockSpec(memory_space=pltpu.VMEM)
    dma = pltpu.SemaphoreType.DMA
    nk = len(CHUNKS)
    return pl.pallas_call(
        kernel,
        out_shape=(
            jax.ShapeDtypeStruct((16, 4096), BF16),
            jax.ShapeDtypeStruct((SLOTS, 8, KVW), BF16),
        ),
        in_specs=[smem] * 3 + [hbm] * 6,
        out_specs=(vmem, vmem),
        scratch_shapes=[
            pltpu.VMEM((SPAN, 512), BF16),
            pltpu.VMEM((SPAN, 256), BF16),
            pltpu.VMEM((KVW, PREFIX), BF16),
            pltpu.VMEM((KVR, 1024), BF16),
            pltpu.VMEM((16, KVW), BF16),
            pltpu.VMEM((16, NL_ROWS, 128), BF16),
            pltpu.VMEM((1024, KVR), BF16),
            pltpu.VMEM((1024, KEYS), BF16),
            pltpu.VMEM((2, 128, KEYS), BF16),
            pltpu.VMEM((16, BLK_ROWS, 128), BF16),
            pltpu.VMEM((2, SPAN, 512), BF16),
            pltpu.VMEM((16, 2, 4, 4, 16, 128), BF16),
            pltpu.VMEM((16, 3, 2, 4, 16, 128), BF16),
            pltpu.VMEM((16, 2, 4, 16, 128), BF16),
            pltpu.VMEM((16, 3, 2, 16, 128), BF16),
            pltpu.VMEM((len(DIRECT), 15, 2, 16, 128), BF16),
            pltpu.VMEM((16, 16, 128), BF16),
            pltpu.VMEM((16, 16, 128), BF16),
            pltpu.VMEM((2, 16, 640), BF16),
            pltpu.VMEM((2, 16, 640), BF16),
            dma((6,)),
            dma((16, nk)),
            dma((16, nk)),
            dma((2,)),
            dma((2,)),
            dma((16, 3)),
            dma((16, 3)),
            dma((16, 3)),
            dma((16, 3)),
            dma((len(DIRECT),)),
            dma((len(DIRECT),)),
            dma((16,)),
            dma((16,)),
            dma((2,)),
        ],
        compiler_params=pltpu.CompilerParams(
            collective_id=0, has_side_effects=True, vmem_limit_bytes=56 * 1024 * 1024
        ),
        cost_estimate=pl.CostEstimate(flops=5_000_000_000, bytes_accessed=6_000_000, transcendentals=2_400_000),
    )(prefix_length, owners, slot_index, query_nope, query_rope, cache, nl, latent_up, out_proj)


def solution(mesh):
    placed = (
        P("grp", "tp"),
        P("grp", "tp"),
        P("grp", None),
        P("grp", "tp", None),
        P("grp"),
        P(None, "tp"),
        P("tp", "grp"),
        P(),
        P(),
    )
    return jax.shard_map(
        body,
        mesh=mesh,
        in_specs=placed,
        out_specs=(P(("grp", "tp"), None), P("grp", "tp", None)),
        check_vma=False,
    )
```

```python
import jax
import jax.numpy as jnp
from jax import lax
from jax.experimental import pallas as pl
from jax.experimental.pallas import tpu as pltpu
from jax.sharding import PartitionSpec as P

NOPE = 128
ROPE = 64
VDIM = 128
KVR = 512
KVW = 576
SLOTS = 4
SPAN = 256
PREFIX = 2048
KEYS = PREFIX + SPAN
HEADS_DEV = 4
GRP = 32
Z = 16
W_ROWS = 512
NL_ROWS = 80
BLK_ROWS = W_ROWS + NL_ROWS
PIECES = ((0, 160), (160, 144), (304, 144), (448, 144))
STEPS = range(9)
NEAR = range(7)
FAR = (7, 8)
MESH = pl.DeviceIdType.MESH
F32 = jnp.float32
BF16 = jnp.bfloat16


def kernel(
    len_ref, own_ref, slot_ref, qn_hbm, qr_hbm, cache_hbm, nl_hbm, up_hbm, w_hbm,
    mixed_ref, dec_ref,
    qn, qr, cache, up, nl, fresh, up_t, kv, ropes, ring, att, part1, part2, p1, mid1, mid2, p2_1, p2_2, p1_1,
    direct1, direct2, res1, res2, res_in1, res_in2, dec, dec_in,
    in_sem, ring_send, ring_recv, first_sem, nl_sem, att_sem, sums_send, p1_recv, p2_recv, direct_recv, res_recv,
    dec_sem,
):
    g = lax.axis_index("grp")
    t = lax.axis_index("tp")
    z, core = g // 2, lax.rem(g, 2)
    x, y = t // 4, lax.rem(t, 4)
    ahead = 1 - 2 * core
    ring_to = {"grp": lax.rem(g + 2 * ahead + GRP, GRP)}
    ring_from = {"grp": lax.rem(g - 2 * ahead + GRP, GRP)}
    sibling = {"grp": g + 1 - 2 * core}
    xs = [lax.rem(x + d, 4) for d in (1, 2, 3)]
    ys = [lax.rem(y + d, 4) for d in (1, 2, 3)]
    x_peers = [{"tp": xx * 4 + y} for xx in xs]
    y_peers = [{"tp": x * 4 + yy} for yy in ys]

    plane = [(dx, dy) for dx in range(4) for dy in range(4)][1:]
    plane_xy = [(lax.rem(x + dx, 4), lax.rem(y + dy, 4)) for dx, dy in plane]
    plane_peers = [{"tp": xx * 4 + yy} for xx, yy in plane_xy]
    partners = [ring_from, ring_to, sibling] + plane_peers
    barrier = pltpu.get_barrier_semaphore()
    for who in partners:
        pl.semaphore_signal(barrier, inc=1, device_id=who, device_id_type=MESH)

    loads = [
        pltpu.make_async_copy(nl_hbm, nl, in_sem.at[0]),
        pltpu.make_async_copy(w_hbm, ring.at[0, pl.ds(0, W_ROWS)], in_sem.at[1]),
        pltpu.make_async_copy(up_hbm, up, in_sem.at[2]),
        pltpu.make_async_copy(cache_hbm, cache, in_sem.at[3]),
        pltpu.make_async_copy(qn_hbm, qn, in_sem.at[4]),
        pltpu.make_async_copy(qr_hbm, qr, in_sem.at[5]),
    ]
    for load in loads:
        load.start()
    loads[0].wait()
    rows = nl[...]
    tiles = [rows[:, k * 128 : (k + 1) * 128] for k in range(4)]
    tiles.append(jnp.concatenate([rows[:, KVR:], jnp.zeros((16, 64), BF16)], axis=1))
    packed = jnp.concatenate(tiles, axis=0)
    ring[0, pl.ds(W_ROWS, NL_ROWS), :] = packed
    fresh[t] = packed
    loads[1].wait()
    pl.semaphore_wait(barrier, len(partners))

    def remote(src, dst, send, recv, who):
        return pltpu.make_async_remote_copy(
            src_ref=src, dst_ref=dst, send_sem=send, recv_sem=recv, device_id=who, device_id_type=MESH
        )

    def hop(b, k):
        at, n = PIECES[k]
        piece = pl.ds(at, n)
        return remote(ring.at[b, piece], ring.at[b + 2, piece], ring_send.at[0], ring_recv.at[b + 2, k], ring_to)

    coming = [(b, k) for b in range(2, 17) for k in range(len(PIECES))]

    def serve(n):
        for _ in range(n * len(PIECES) // 2):
            b, k = coming.pop(0)
            hop(b - 2, k).wait_recv()
            if b < 15:
                hop(b, k).start()

    first = remote(ring.at[0], ring.at[1], first_sem.at[0], first_sem.at[1], sibling)

    def new_rows(i):
        return remote(fresh.at[t], fresh.at[t], nl_sem.at[0], nl_sem.at[1], plane_peers[i])

    others = fresh.at[pl.ds(0, 15)]
    all_new_rows = remote(others, others, nl_sem.at[0], nl_sem.at[1], plane_peers[0])

    for k in range(len(PIECES)):
        hop(0, k).start()
    first.start()
    for i in range(15):
        new_rows(i).start()

    def look(n, codes):
        u, i = n // 2, lax.rem(n, 2)
        b = jnp.where(u > 0, u + 1, 0)
        plane = lax.rem(z - ahead * (b // 2) + Z, Z)
        block = 2 * (2 * plane + lax.rem(core + b, 2)) + i
        owner, place = own_ref[block], slot_ref[block]
        wanted = [(who, s) for who in (g, g + 1 - 2 * core) for s in range(SLOTS)]
        return tuple(
            jnp.where(jnp.logical_and(owner == who, place == s), 2 * b + i, old)
            for (who, s), old in zip(wanted, codes, strict=True)
        )

    codes = lax.fori_loop(0, 2 * Z, look, (jnp.int32(-1),) * (2 * SLOTS))

    def rope_rows(rope, at, n):
        zero = jnp.zeros((64, n), BF16)
        ropes[0, :, pl.ds(at, n)] = jnp.concatenate([rope, zero], axis=0)
        ropes[1, :, pl.ds(at, n)] = jnp.concatenate([zero, rope], axis=0)

    for i in (2, 3):
        loads[i].wait()

    up_t[...] = up[...].T

    def prefix_keys(i, _):
        at = pl.multiple_of(i * 256, 256)
        kv[:, pl.ds(at, 256)] = jnp.dot(
            up_t[...], cache[pl.ds(0, KVR), pl.ds(at, 256)], preferred_element_type=F32
        ).astype(BF16)
        rope_rows(cache[pl.ds(KVR, ROPE), pl.ds(at, 256)], at, 256)
        return _

    lax.fori_loop(0, 2, prefix_keys, 0)
    first.wait_recv()
    for k in range(len(PIECES)):
        hop(1, k).start()
    lax.fori_loop(2, 5, prefix_keys, 0)
    serve(1)
    lax.fori_loop(5, 8, prefix_keys, 0)
    serve(2)
    all_new_rows.wait_recv()
    new = fresh[...].reshape(16, 5, 16, 128)
    new = [new[:, k].reshape(SPAN, 128) for k in range(5)]
    kv[:, pl.ds(PREFIX, SPAN)] = lax.dot_general(
        up_t[...], jnp.concatenate(new[:4], axis=1), (((1,), (1,)), ((), ())), preferred_element_type=F32
    ).astype(BF16)
    rope_rows(new[4].T[:ROPE], PREFIX, SPAN)

    for i in (4, 5):
        loads[i].wait()
    to_bits = (NOPE + ROPE) ** -0.5 * 1.4426950408889634
    col = lax.broadcasted_iota(jnp.int32, (1, PREFIX), 1)
    old_bias = jnp.where(col < len_ref[0], 0.0, -1e30).astype(F32)
    row = lax.broadcasted_iota(jnp.int32, (SPAN, SPAN), 0)
    key = lax.broadcasted_iota(jnp.int32, (SPAN, SPAN), 1)
    token = ((key // 8) % 2) * 128 + (key // 16) * 8 + key % 8
    new_bias = jnp.where(token <= row, 0.0, -1e30).astype(F32)

    ones = jnp.ones((VDIM, KEYS), BF16)

    def weights(h):
        k = jnp.concatenate([kv[h * 256 : h * 256 + NOPE], ropes[h % 2]], axis=0)
        pair = h // 2
        q = jnp.concatenate([qn[:, h * 128 : (h + 1) * 128], qr[:, pair * 128 : (pair + 1) * 128]], axis=1)
        s = jnp.dot((q.astype(F32) * to_bits).astype(BF16), k, preferred_element_type=F32)
        s = jnp.concatenate([s[:, :PREFIX] + old_bias, s[:, PREFIX:] + new_bias], axis=1)
        return jnp.exp2(s - jnp.max(s, axis=1, keepdims=True)).astype(BF16)

    def attend(h, e):
        v = jnp.concatenate([kv[h * 256 + NOPE : (h + 1) * 256], ones], axis=0)
        o = lax.dot_general(e, v, (((1,), (1,)), ((), ())), preferred_element_type=F32)
        att[0, :, h * 128 : (h + 1) * 128] = (o[:, :VDIM] / o[:, VDIM:]).astype(BF16)

    def swap(h):
        cols = pl.ds(h * 128, 128)
        return remote(att.at[0, :, cols], att.at[1, :, cols], att_sem.at[0, h], att_sem.at[1, h], sibling)

    serve(2)
    e = weights(0)
    for h in range(1, HEADS_DEV):
        serve(1)
        attend(h - 1, e)
        e = weights(h)
        swap(h - 1).start()
        serve(1)
    attend(HEADS_DEV - 1, e)
    swap(HEADS_DEV - 1).start()
    serve(1)

    def wide(s):
        return 1 <= s <= 7

    def part(s, *at):
        return part2.at[(s - 1, *at)] if wide(s) else part1.at[(s // 8, *at)]

    def mid(s, *at):
        return mid2.at[(s - 1, *at)] if wide(s) else mid1.at[at]

    def first_in(s, *at):
        return p1.at[(s - 1, *at)] if wide(s) else p1_1.at[at]

    def second_in(s, *at):
        return p2_2.at[(s - 1, *at)] if wide(s) else p2_1.at[at]

    def direct_in(s, *at):
        return direct2.at[at] if wide(s) else direct1.at[at]

    def res(s):
        return res2.at[s - 1] if wide(s) else res1.at[s // 8]

    def res_in(s):
        return res_in2.at[s - 1] if wide(s) else res_in1.at[s // 8]

    def out_first(s, i):
        src = part(s, slice(None), slice(None), ys[i]) if s % 2 else part(s, slice(None), xs[i])
        who = y_peers[i] if s % 2 else x_peers[i]
        return remote(src, first_in(s, i), sums_send.at[int(wide(s))], p1_recv.at[s], who)

    def out_second(s, i):
        src = mid(s, slice(None), xs[i] if s % 2 else ys[i])
        who = x_peers[i] if s % 2 else y_peers[i]
        return remote(src, second_in(s, i), sums_send.at[2 + int(wide(s))], p2_recv.at[s], who)

    def out_direct(s, i):
        xx, yy = plane_xy[i]
        src = part(s, slice(None), xx, yy)
        return remote(src, direct_in(s, i), sums_send.at[4 + int(wide(s))], direct_recv.at[int(wide(s))], plane_peers[i])

    def out_res(s):
        return remote(res(s), res_in(s), sums_send.at[6 + int(wide(s))], res_recv.at[s], sibling)

    def arrived(ref, sem):
        remote(ref, ref, sem, sem, sibling).wait_recv()

    def left(ref, sem):
        remote(ref, ref, sem, sem, sibling).wait_send()

    def project(s):
        w = [ring[b, pl.ds(0, W_ROWS), :] for b in ((2 * s, 2 * s + 1) if wide(s) else (2 * s,))]
        a = att[...].reshape(2 * SPAN, W_ROWS)
        o = jnp.dot(a, jnp.concatenate(w, axis=1), preferred_element_type=F32).astype(BF16)
        part(s)[...] = o.reshape(2, 4, 4, 16, 128 * len(w))
        for i in range(15 if s in FAR else 3):
            (out_direct if s in FAR else out_first)(s, i).start()

    def add(own, terms):
        total = own[...].astype(F32)
        for term in terms:
            total += term[...].astype(F32)
        return total.astype(BF16)

    def first_sum(s):
        arrived(first_in(s), p1_recv.at[s])
        own = part(s, slice(None), slice(None), y) if s % 2 else part(s, slice(None), x)
        mid(s)[...] = add(own, [first_in(s, i) for i in range(3)])
        for i in range(3):
            out_second(s, i).start()

    def store(s, rows, core, ahead):
        plane = lax.rem(z - ahead * s + Z, Z)
        for n in range(2 if wide(s) else 1):
            at = pl.multiple_of((2 * plane + lax.rem(core + n, 2)) * 128, 128)
            mixed_ref[:, pl.ds(at, 128)] = rows[:, n * 128 : (n + 1) * 128]

    def deliver(s, total):
        res(s)[...] = total[1]
        out_res(s).start()
        store(s, total[0], core, ahead)

    def second_sum(s):
        arrived(second_in(s), p2_recv.at[s])
        own = mid(s, slice(None), x if s % 2 else y)
        deliver(s, add(own, [second_in(s, i) for i in range(3)]))

    def direct_sum(s):
        arrived(direct_in(s), direct_recv.at[int(wide(s))])
        deliver(s, add(part(s, slice(None), x, y), [direct_in(s, i) for i in range(15)]))

    def collect(s):
        arrived(res_in(s), res_recv.at[s])
        store(s, res_in(s)[...], 1 - core, -ahead)

    for h in range(HEADS_DEV):
        swap(h).wait_recv()
    serve(1)
    project(0)
    project(1)
    serve(1)
    project(2)
    project(3)
    serve(2)
    project(4)
    serve(2)
    first_sum(0)
    serve(1)
    first_sum(1)
    serve(1)
    project(5)
    serve(1)
    first_sum(2)
    serve(1)
    first_sum(3)
    serve(2)
    project(6)
    first_sum(4)
    second_sum(0)
    serve(1)
    second_sum(1)
    second_sum(2)
    serve(1)
    first_sum(5)
    serve(1)
    second_sum(3)
    serve(1)
    project(7)
    second_sum(4)
    serve(2)
    project(8)
    first_sum(6)
    second_sum(5)
    assert not coming

    def pick(code):
        got = ring[jnp.maximum(code, 0) // 2, pl.ds(W_ROWS, NL_ROWS), :].reshape(5, 16, 128).astype(F32)
        got = jnp.where(lax.rem(jnp.maximum(code, 0), 2) == 0, got[:, :8], got[:, 8:])
        got = jnp.where(code >= 0, got, 0.0)
        return jnp.concatenate([got[k] for k in range(5)], axis=1)

    for s in range(0, SLOTS, 2):
        both = jnp.concatenate([pick(codes[SLOTS + s]), pick(codes[SLOTS + s + 1])], axis=0)
        dec[s // 2] = both.astype(BF16)
    swap_dec = remote(dec, dec_in, dec_sem.at[0], dec_sem.at[1], sibling)
    swap_dec.start()
    mine = [pick(codes[s]) for s in range(SLOTS)]
    swap_dec.wait_recv()
    for s in range(SLOTS):
        other = dec_in[s // 2].astype(F32)[(s % 2) * 8 : (s % 2) * 8 + 8]
        dec_ref[s] = (mine[s] + other)[:, :KVW].astype(BF16)

    for s in (0, 1, 2, 3, 4, 5):
        collect(s)
    direct_sum(7)
    second_sum(6)
    collect(7)
    collect(6)
    direct_sum(8)
    collect(8)

    left(ring.at[pl.ds(2, 15)], ring_send.at[0])
    first.wait_send()
    all_new_rows.wait_send()
    for h in range(HEADS_DEV):
        swap(h).wait_send()
    swap_dec.wait_send()
    for n, ref in enumerate((p1_1, p1, p2_1, p2_2, direct1, direct2, res_in1, res_in2)):
        left(ref, sums_send.at[n])


def body(query_nope, query_rope, latent_cache, new_latent, prefix_length, latent_up, out_proj, owners, slot_index):
    nl = new_latent.reshape(16, KVW)
    cache = latent_cache.T
    smem = pl.BlockSpec(memory_space=pltpu.SMEM)
    hbm = pl.BlockSpec(memory_space=pl.ANY)
    vmem = pl.BlockSpec(memory_space=pltpu.VMEM)
    dma = pltpu.SemaphoreType.DMA
    nk = len(PIECES)
    return pl.pallas_call(
        kernel,
        out_shape=(
            jax.ShapeDtypeStruct((16, 4096), BF16),
            jax.ShapeDtypeStruct((SLOTS, 8, KVW), BF16),
        ),
        in_specs=[smem] * 3 + [hbm] * 6,
        out_specs=(vmem, vmem),
        scratch_shapes=[
            pltpu.VMEM((SPAN, 512), BF16),
            pltpu.VMEM((SPAN, 256), BF16),
            pltpu.VMEM((KVW, PREFIX), BF16),
            pltpu.VMEM((KVR, 1024), BF16),
            pltpu.VMEM((16, KVW), BF16),
            pltpu.VMEM((16, NL_ROWS, 128), BF16),
            pltpu.VMEM((1024, KVR), BF16),
            pltpu.VMEM((1024, KEYS), BF16),
            pltpu.VMEM((2, 128, KEYS), BF16),
            pltpu.VMEM((17, BLK_ROWS, 128), BF16),
            pltpu.VMEM((2, SPAN, 512), BF16),
            pltpu.VMEM((2, 2, 4, 4, 16, 128), BF16),
            pltpu.VMEM((7, 2, 4, 4, 16, 256), BF16),
            pltpu.VMEM((6, 3, 2, 4, 16, 256), BF16),
            pltpu.VMEM((2, 4, 16, 128), BF16),
            pltpu.VMEM((6, 2, 4, 16, 256), BF16),
            pltpu.VMEM((3, 2, 16, 128), BF16),
            pltpu.VMEM((6, 3, 2, 16, 256), BF16),
            pltpu.VMEM((3, 2, 4, 16, 128), BF16),
            pltpu.VMEM((15, 2, 16, 128), BF16),
            pltpu.VMEM((15, 2, 16, 256), BF16),
            pltpu.VMEM((2, 16, 128), BF16),
            pltpu.VMEM((7, 16, 256), BF16),
            pltpu.VMEM((2, 16, 128), BF16),
            pltpu.VMEM((7, 16, 256), BF16),
            pltpu.VMEM((2, 16, 640), BF16),
            pltpu.VMEM((2, 16, 640), BF16),
            dma((6,)),
            dma((1,)),
            dma((17, nk)),
            dma((2,)),
            dma((2,)),
            dma((2, HEADS_DEV)),
            dma((8,)),
            dma((7,)),
            dma((7,)),
            dma((2,)),
            dma((9,)),
            dma((2,)),
        ],
        compiler_params=pltpu.CompilerParams(
            collective_id=0, has_side_effects=True, vmem_limit_bytes=56 * 1024 * 1024
        ),
        cost_estimate=pl.CostEstimate(flops=5_000_000_000, bytes_accessed=6_000_000, transcendentals=2_400_000),
    )(prefix_length, owners, slot_index, query_nope, query_rope, cache, nl, latent_up, out_proj)


def solution(mesh):
    placed = (
        P("grp", "tp"),
        P("grp", "tp"),
        P("grp", None),
        P("grp", "tp", None),
        P("grp"),
        P(None, "tp"),
        P("tp", "grp"),
        P(),
        P(),
    )
    return jax.shard_map(
        body,
        mesh=mesh,
        in_specs=placed,
        out_specs=(P(("grp", "tp"), None), P("grp", "tp", None)),
        check_vma=False,
    )
```

```python
import jax
import jax.numpy as jnp
from jax import lax
from jax.experimental import pallas as pl
from jax.experimental.pallas import tpu as pltpu
from jax.sharding import PartitionSpec as P

NOPE = 128
ROPE = 64
VDIM = 128
KVR = 512
KVW = 576
SLOTS = 4
SPAN = 256
PREFIX = 2048
KEYS = PREFIX + SPAN
HEADS_DEV = 4
GRP = 32
Z = 16
W_ROWS = 512
NL_ROWS = 80
BLK_ROWS = W_ROWS + NL_ROWS
PIECES = ((0, 304), (304, 288))
NEAR = range(7)
FAR = (14, 15, 16)
MESH = pl.DeviceIdType.MESH
F32 = jnp.float32
BF16 = jnp.bfloat16


def kernel(
    len_ref, own_ref, slot_ref, qn_hbm, qr_hbm, cache_hbm, nl_hbm, up_hbm, w_hbm,
    mixed_ref, dec_ref,
    qn, qr, cache, up, nl, fresh, up_t, kv, ropes, ring, att, part1, part2, p1_1, p1_2, mid1, mid2, p2_1, p2_2,
    res1, res2, res_in1, res_in2, part_far, direct, res_far, res_in_far, dec, dec_in,
    in_sem, ring_send, ring_recv, first_sem, nl_sem, att_sem, sums_send, p1_recv, p2_recv, res_recv, far_send, far_recv,
    dec_sem,
):
    g = lax.axis_index("grp")
    t = lax.axis_index("tp")
    z, core = g // 2, lax.rem(g, 2)
    x, y = t // 4, lax.rem(t, 4)
    ahead = 1 - 2 * core
    ring_to = {"grp": lax.rem(g + 2 * ahead + GRP, GRP)}
    ring_from = {"grp": lax.rem(g - 2 * ahead + GRP, GRP)}
    sibling = {"grp": g + 1 - 2 * core}
    xs = [lax.rem(x + d, 4) for d in (2, 1, 3)]
    ys = [lax.rem(y + d, 4) for d in (2, 1, 3)]
    x_peers = [{"tp": xx * 4 + y} for xx in xs]
    y_peers = [{"tp": x * 4 + yy} for yy in ys]

    plane = [(dx, dy) for dx in range(4) for dy in range(4)][1:]
    plane.sort(key=lambda d: -min(d[0], 4 - d[0]) - min(d[1], 4 - d[1]))
    plane_xy = [(lax.rem(x + dx, 4), lax.rem(y + dy, 4)) for dx, dy in plane]
    plane_peers = [{"tp": xx * 4 + yy} for xx, yy in plane_xy]
    partners = [ring_from, ring_to, sibling] + plane_peers
    barrier = pltpu.get_barrier_semaphore()
    for who in partners:
        pl.semaphore_signal(barrier, inc=1, device_id=who, device_id_type=MESH)

    loads = [
        pltpu.make_async_copy(nl_hbm, nl, in_sem.at[0]),
        pltpu.make_async_copy(w_hbm, ring.at[0, pl.ds(0, W_ROWS)], in_sem.at[1]),
        pltpu.make_async_copy(up_hbm, up, in_sem.at[2]),
        pltpu.make_async_copy(cache_hbm, cache, in_sem.at[3]),
        pltpu.make_async_copy(qn_hbm, qn, in_sem.at[4]),
        pltpu.make_async_copy(qr_hbm, qr, in_sem.at[5]),
    ]
    for load in loads:
        load.start()
    loads[0].wait()
    rows = nl[...]
    tiles = [rows[:, k * 128 : (k + 1) * 128] for k in range(4)]
    tiles.append(jnp.concatenate([rows[:, KVR:], jnp.zeros((16, 64), BF16)], axis=1))
    packed = jnp.concatenate(tiles, axis=0)
    ring[0, pl.ds(W_ROWS, NL_ROWS), :] = packed
    fresh[t] = packed
    loads[1].wait()
    pl.semaphore_wait(barrier, len(partners))

    def remote(src, dst, send, recv, who):
        return pltpu.make_async_remote_copy(
            src_ref=src, dst_ref=dst, send_sem=send, recv_sem=recv, device_id=who, device_id_type=MESH
        )

    def hop(b, k):
        at, n = PIECES[k]
        piece = pl.ds(at, n)
        return remote(ring.at[b, piece], ring.at[b + 2, piece], ring_send.at[0], ring_recv.at[b + 2, k], ring_to)

    coming = [(b, k) for b in range(2, 17) for k in range(len(PIECES))]

    def serve(n):
        for _ in range(n * len(PIECES) // 2):
            b, k = coming.pop(0)
            hop(b - 2, k).wait_recv()
            if b < 15:
                hop(b, k).start()

    first = remote(ring.at[0], ring.at[1], first_sem.at[0], first_sem.at[1], sibling)

    def new_rows(i):
        return remote(fresh.at[t], fresh.at[t], nl_sem.at[0], nl_sem.at[1], plane_peers[i])

    others = fresh.at[pl.ds(0, 15)]
    all_new_rows = remote(others, others, nl_sem.at[0], nl_sem.at[1], plane_peers[0])

    for k in range(len(PIECES)):
        hop(0, k).start()
    first.start()
    for i in range(15):
        new_rows(i).start()

    def look(n, codes):
        u, i = n // 2, lax.rem(n, 2)
        b = jnp.where(u > 0, u + 1, 0)
        plane = lax.rem(z - ahead * (b // 2) + Z, Z)
        block = 2 * (2 * plane + lax.rem(core + b, 2)) + i
        owner, place = own_ref[block], slot_ref[block]
        wanted = [(who, s) for who in (g, g + 1 - 2 * core) for s in range(SLOTS)]
        return tuple(
            jnp.where(jnp.logical_and(owner == who, place == s), 2 * b + i, old)
            for (who, s), old in zip(wanted, codes, strict=True)
        )

    codes = lax.fori_loop(0, 2 * Z, look, (jnp.int32(-1),) * (2 * SLOTS))

    def rope_rows(rope, at, n):
        zero = jnp.zeros((64, n), BF16)
        ropes[0, :, pl.ds(at, n)] = jnp.concatenate([rope, zero], axis=0)
        ropes[1, :, pl.ds(at, n)] = jnp.concatenate([zero, rope], axis=0)

    for i in (2, 3):
        loads[i].wait()

    up_t[...] = up[...].T

    def prefix_keys(i, _):
        at = pl.multiple_of(i * 256, 256)
        kv[:, pl.ds(at, 256)] = jnp.dot(
            up_t[...], cache[pl.ds(0, KVR), pl.ds(at, 256)], preferred_element_type=F32
        ).astype(BF16)
        rope_rows(cache[pl.ds(KVR, ROPE), pl.ds(at, 256)], at, 256)
        return _

    lax.fori_loop(0, 2, prefix_keys, 0)
    first.wait_recv()
    for k in range(len(PIECES)):
        hop(1, k).start()
    lax.fori_loop(2, 5, prefix_keys, 0)
    serve(1)
    lax.fori_loop(5, 8, prefix_keys, 0)
    serve(2)
    all_new_rows.wait_recv()
    new = fresh[...].reshape(16, 5, 16, 128)
    new = [new[:, k].reshape(SPAN, 128) for k in range(5)]
    kv[:, pl.ds(PREFIX, SPAN)] = lax.dot_general(
        up_t[...], jnp.concatenate(new[:4], axis=1), (((1,), (1,)), ((), ())), preferred_element_type=F32
    ).astype(BF16)
    rope_rows(new[4].T[:ROPE], PREFIX, SPAN)

    for i in (4, 5):
        loads[i].wait()
    to_bits = (NOPE + ROPE) ** -0.5 * 1.4426950408889634
    col = lax.broadcasted_iota(jnp.int32, (1, PREFIX), 1)
    old_bias = jnp.where(col < len_ref[0], 0.0, -1e30).astype(F32)
    row = lax.broadcasted_iota(jnp.int32, (SPAN, SPAN), 0)
    key = lax.broadcasted_iota(jnp.int32, (SPAN, SPAN), 1)
    token = ((key // 8) % 2) * 128 + (key // 16) * 8 + key % 8
    new_bias = jnp.where(token <= row, 0.0, -1e30).astype(F32)

    ones = jnp.ones((VDIM, KEYS), BF16)

    def weights(h):
        k = jnp.concatenate([kv[h * 256 : h * 256 + NOPE], ropes[h % 2]], axis=0)
        pair = h // 2
        q = jnp.concatenate([qn[:, h * 128 : (h + 1) * 128], qr[:, pair * 128 : (pair + 1) * 128]], axis=1)
        s = jnp.dot((q.astype(F32) * to_bits).astype(BF16), k, preferred_element_type=F32)
        s = jnp.concatenate([s[:, :PREFIX] + old_bias, s[:, PREFIX:] + new_bias], axis=1)
        return jnp.exp2(s - jnp.max(s, axis=1, keepdims=True)).astype(BF16)

    def attend(h, e):
        v = jnp.concatenate([kv[h * 256 + NOPE : (h + 1) * 256], ones], axis=0)
        o = lax.dot_general(e, v, (((1,), (1,)), ((), ())), preferred_element_type=F32)
        att[0, :, h * 128 : (h + 1) * 128] = (o[:, :VDIM] / o[:, VDIM:]).astype(BF16)

    def swap(h):
        cols = pl.ds(h * 128, 128)
        return remote(att.at[0, :, cols], att.at[1, :, cols], att_sem.at[0, h], att_sem.at[1, h], sibling)

    serve(2)
    e = weights(0)
    for h in range(1, HEADS_DEV):
        serve(1)
        attend(h - 1, e)
        e = weights(h)
        swap(h - 1).start()
        serve(1)
    attend(HEADS_DEV - 1, e)
    swap(HEADS_DEV - 1).start()
    serve(1)

    def part(s, *at):
        return part2.at[(s - 1, *at)] if s else part1.at[at]

    def mid(s, *at):
        return mid2.at[(s - 1, *at)] if s else mid1.at[at]

    def first_in(s, *at):
        return p1_2.at[(s - 1, *at)] if s else p1_1.at[at]

    def second_in(s, *at):
        return p2_2.at[(s - 1, *at)] if s else p2_1.at[at]

    def res(s):
        return res2.at[s - 1] if s else res1

    def res_in(s):
        return res_in2.at[s - 1] if s else res_in1

    def out_first(s, i):
        src = part(s, slice(None), slice(None), ys[i]) if s % 2 else part(s, slice(None), xs[i])
        who = y_peers[i] if s % 2 else x_peers[i]
        return remote(src, first_in(s, i), sums_send.at[int(s > 0)], p1_recv.at[s], who)

    def out_second(s, i):
        src = mid(s, slice(None), xs[i] if s % 2 else ys[i])
        who = x_peers[i] if s % 2 else y_peers[i]
        return remote(src, second_in(s, i), sums_send.at[2 + int(s > 0)], p2_recv.at[s], who)

    def out_res(s):
        return remote(res(s), res_in(s), sums_send.at[4 + int(s > 0)], res_recv.at[s], sibling)

    def out_far(f, i):
        xx, yy = plane_xy[i]
        return remote(part_far.at[f, :, xx, yy], direct.at[f, i], far_send.at[0, f], far_recv.at[0, f], plane_peers[i])

    def out_res_far(f):
        return remote(res_far.at[f], res_in_far.at[f], far_send.at[1, f], far_recv.at[1, f], sibling)

    def arrived(ref, sem):
        remote(ref, ref, sem, sem, sibling).wait_recv()

    def left(ref, sem):
        remote(ref, ref, sem, sem, sibling).wait_send()

    def times(blocks):
        w = [ring[b, pl.ds(0, W_ROWS), :] for b in blocks]
        a = att[...].reshape(2 * SPAN, W_ROWS)
        o = jnp.dot(a, jnp.concatenate(w, axis=1), preferred_element_type=F32).astype(BF16)
        return o.reshape(2, 4, 4, 16, 128 * len(w))

    def project(s):
        part(s)[...] = times((2 * s, 2 * s + 1) if s else (0,))
        for i in range(3):
            out_first(s, i).start()

    def project_far(f):
        part_far[f] = times((FAR[f],))
        for i in range(15):
            out_far(f, i).start()

    def add(own, terms):
        total = own[...].astype(F32)
        for term in terms:
            total += term[...].astype(F32)
        return total.astype(BF16)

    def first_sum(s):
        arrived(first_in(s), p1_recv.at[s])
        own = part(s, slice(None), slice(None), y) if s % 2 else part(s, slice(None), x)
        mid(s)[...] = add(own, [first_in(s, i) for i in range(3)])
        for i in range(3):
            out_second(s, i).start()

    def store(b, rows, core, ahead):
        plane = lax.rem(z - ahead * (b // 2) + Z, Z)
        for n in range(rows.shape[1] // 128):
            at = pl.multiple_of((2 * plane + lax.rem(core + b + n, 2)) * 128, 128)
            mixed_ref[:, pl.ds(at, 128)] = rows[:, n * 128 : (n + 1) * 128]

    def second_sum(s):
        arrived(second_in(s), p2_recv.at[s])
        own = mid(s, slice(None), x if s % 2 else y)
        total = add(own, [second_in(s, i) for i in range(3)])
        res(s)[...] = total[1]
        out_res(s).start()
        store(2 * s, total[0], core, ahead)

    def direct_sum(f):
        arrived(direct.at[f], far_recv.at[0, f])
        total = add(part_far.at[f, :, x, y], [direct.at[f, i] for i in range(15)])
        res_far[f] = total[1]
        out_res_far(f).start()
        store(FAR[f], total[0], core, ahead)

    def collect(s):
        arrived(res_in(s), res_recv.at[s])
        store(2 * s, res_in(s)[...], 1 - core, -ahead)

    def collect_far(f):
        arrived(res_in_far.at[f], far_recv.at[1, f])
        store(FAR[f], res_in_far[f], 1 - core, -ahead)

    for h in range(HEADS_DEV):
        swap(h).wait_recv()
    serve(1)
    project(0)
    project(1)
    serve(1)
    project(2)
    project(3)
    serve(2)
    project(4)
    serve(2)
    first_sum(0)
    serve(1)
    first_sum(1)
    serve(1)
    project(5)
    serve(1)
    first_sum(2)
    serve(1)
    first_sum(3)
    serve(2)
    project(6)
    first_sum(4)
    second_sum(0)
    serve(1)
    second_sum(1)
    second_sum(2)
    serve(1)
    project_far(0)
    first_sum(5)
    second_sum(3)
    serve(2)
    project_far(1)
    first_sum(6)
    second_sum(4)
    serve(2)
    project_far(2)
    second_sum(5)
    assert not coming

    def pick(code):
        got = ring[jnp.maximum(code, 0) // 2, pl.ds(W_ROWS, NL_ROWS), :].reshape(5, 16, 128).astype(F32)
        got = jnp.where(lax.rem(jnp.maximum(code, 0), 2) == 0, got[:, :8], got[:, 8:])
        got = jnp.where(code >= 0, got, 0.0)
        return jnp.concatenate([got[k] for k in range(5)], axis=1)

    for s in range(0, SLOTS, 2):
        both = jnp.concatenate([pick(codes[SLOTS + s]), pick(codes[SLOTS + s + 1])], axis=0)
        dec[s // 2] = both.astype(BF16)
    swap_dec = remote(dec, dec_in, dec_sem.at[0], dec_sem.at[1], sibling)
    swap_dec.start()
    mine = [pick(codes[s]) for s in range(SLOTS)]
    swap_dec.wait_recv()
    for s in range(SLOTS):
        other = dec_in[s // 2].astype(F32)[(s % 2) * 8 : (s % 2) * 8 + 8]
        dec_ref[s] = (mine[s] + other)[:, :KVW].astype(BF16)

    for s in range(6):
        collect(s)
    direct_sum(0)
    direct_sum(1)
    second_sum(6)
    collect_far(0)
    collect_far(1)
    collect(6)
    left(ring.at[pl.ds(2, 15)], ring_send.at[0])
    first.wait_send()
    all_new_rows.wait_send()
    for h in range(HEADS_DEV):
        swap(h).wait_send()
    swap_dec.wait_send()
    for n, ref in enumerate((p1_1, p1_2, p2_1, p2_2, res_in1, res_in2)):
        left(ref, sums_send.at[n])
    for f in range(3):
        left(direct.at[f], far_send.at[0, f])
    direct_sum(2)
    collect_far(2)
    for f in range(3):
        left(res_in_far.at[f], far_send.at[1, f])


def body(query_nope, query_rope, latent_cache, new_latent, prefix_length, latent_up, out_proj, owners, slot_index):
    nl = new_latent.reshape(16, KVW)
    cache = latent_cache.T
    smem = pl.BlockSpec(memory_space=pltpu.SMEM)
    hbm = pl.BlockSpec(memory_space=pl.ANY)
    vmem = pl.BlockSpec(memory_space=pltpu.VMEM)
    dma = pltpu.SemaphoreType.DMA
    nk = len(PIECES)
    return pl.pallas_call(
        kernel,
        out_shape=(
            pltpu.VMEM((16, 4096), BF16),
            pltpu.VMEM((SLOTS, 8, KVW), BF16),
        ),
        in_specs=[smem] * 3 + [hbm] * 6,
        out_specs=(vmem, vmem),
        scratch_shapes=[
            pltpu.VMEM((SPAN, 512), BF16),
            pltpu.VMEM((SPAN, 256), BF16),
            pltpu.VMEM((KVW, PREFIX), BF16),
            pltpu.VMEM((KVR, 1024), BF16),
            pltpu.VMEM((16, KVW), BF16),
            pltpu.VMEM((16, NL_ROWS, 128), BF16),
            pltpu.VMEM((1024, KVR), BF16),
            pltpu.VMEM((1024, KEYS), BF16),
            pltpu.VMEM((2, 128, KEYS), BF16),
            pltpu.VMEM((17, BLK_ROWS, 128), BF16),
            pltpu.VMEM((2, SPAN, 512), BF16),
            pltpu.VMEM((2, 4, 4, 16, 128), BF16),
            pltpu.VMEM((6, 2, 4, 4, 16, 256), BF16),
            pltpu.VMEM((3, 2, 4, 16, 128), BF16),
            pltpu.VMEM((6, 3, 2, 4, 16, 256), BF16),
            pltpu.VMEM((2, 4, 16, 128), BF16),
            pltpu.VMEM((6, 2, 4, 16, 256), BF16),
            pltpu.VMEM((3, 2, 16, 128), BF16),
            pltpu.VMEM((6, 3, 2, 16, 256), BF16),
            pltpu.VMEM((16, 128), BF16),
            pltpu.VMEM((6, 16, 256), BF16),
            pltpu.VMEM((16, 128), BF16),
            pltpu.VMEM((6, 16, 256), BF16),
            pltpu.VMEM((3, 2, 4, 4, 16, 128), BF16),
            pltpu.VMEM((3, 15, 2, 16, 128), BF16),
            pltpu.VMEM((3, 16, 128), BF16),
            pltpu.VMEM((3, 16, 128), BF16),
            pltpu.VMEM((2, 16, 640), BF16),
            pltpu.VMEM((2, 16, 640), BF16),
            dma((6,)),
            dma((1,)),
            dma((17, nk)),
            dma((2,)),
            dma((2,)),
            dma((2, HEADS_DEV)),
            dma((6,)),
            dma((7,)),
            dma((7,)),
            dma((7,)),
            dma((2, 3)),
            dma((2, 3)),
            dma((2,)),
        ],
        compiler_params=pltpu.CompilerParams(
            collective_id=0, has_side_effects=True, vmem_limit_bytes=56 * 1024 * 1024
        ),
        cost_estimate=pl.CostEstimate(flops=5_000_000_000, bytes_accessed=6_000_000, transcendentals=2_400_000),
    )(prefix_length, owners, slot_index, query_nope, query_rope, cache, nl, latent_up, out_proj)


def solution(mesh):
    placed = (
        P("grp", "tp"),
        P("grp", "tp"),
        P("grp", None),
        P("grp", "tp", None),
        P("grp"),
        P(None, "tp"),
        P("tp", "grp"),
        P(),
        P(),
    )
    return jax.shard_map(
        body,
        mesh=mesh,
        in_specs=placed,
        out_specs=(P(("grp", "tp"), None), P("grp", "tp", None)),
        check_vma=False,
    )
```

```python
import jax
import jax.numpy as jnp
from jax import lax
from jax.experimental import pallas as pl
from jax.experimental.pallas import tpu as pltpu
from jax.sharding import PartitionSpec as P

NOPE = 128
ROPE = 64
VDIM = 128
KVR = 512
KVW = 576
SLOTS = 4
SPAN = 256
PREFIX = 2048
KEYS = PREFIX + SPAN
HEADS_DEV = 4
GRP = 32
Z = 16
W_ROWS = 512
NL_ROWS = 80
BLK_ROWS = W_ROWS + NL_ROWS
PIECES = ((0, 304), (304, 288))
NEAR = range(7)
FAR = (14, 15, 16)
MESH = pl.DeviceIdType.MESH
F32 = jnp.float32
BF16 = jnp.bfloat16


def kernel(
    len_hbm, own_hbm, slot_hbm, qn_hbm, qr_hbm, cache_hbm, nl_hbm, up_hbm, w_hbm,
    mixed_ref, dec_ref,
    len_ref, own_ref, slot_ref, qn, qr, cache, up, nl, fresh, up_t, kv, ropes, ring, att, part1, part2, p1_1, p1_2, mid1, mid2, p2_1, p2_2,
    res1, res2, res_in1, res_in2, part_far, direct, res_far, res_in_far, dec, dec_in,
    in_sem, ring_send, ring_recv, first_sem, nl_sem, att_sem, sums_send, p1_recv, p2_recv, res_recv, far_send, far_recv,
    dec_sem,
):
    g = lax.axis_index("grp")
    t = lax.axis_index("tp")
    z, core = g // 2, lax.rem(g, 2)
    x, y = t // 4, lax.rem(t, 4)
    ahead = 1 - 2 * core
    ring_to = {"grp": lax.rem(g + 2 * ahead + GRP, GRP)}
    ring_from = {"grp": lax.rem(g - 2 * ahead + GRP, GRP)}
    sibling = {"grp": g + 1 - 2 * core}
    xs = [lax.rem(x + d, 4) for d in (2, 1, 3)]
    ys = [lax.rem(y + d, 4) for d in (2, 1, 3)]
    x_peers = [{"tp": xx * 4 + y} for xx in xs]
    y_peers = [{"tp": x * 4 + yy} for yy in ys]

    plane = [(dx, dy) for dx in range(4) for dy in range(4)][1:]
    plane.sort(key=lambda d: -min(d[0], 4 - d[0]) - min(d[1], 4 - d[1]))
    plane_xy = [(lax.rem(x + dx, 4), lax.rem(y + dy, 4)) for dx, dy in plane]
    plane_peers = [{"tp": xx * 4 + yy} for xx, yy in plane_xy]
    partners = plane_peers + [ring_from, ring_to, sibling]

    loads = [
        pltpu.make_async_copy(nl_hbm, nl, in_sem.at[0]),
        pltpu.make_async_copy(w_hbm, ring.at[0, pl.ds(0, W_ROWS)], in_sem.at[1]),
        pltpu.make_async_copy(up_hbm, up, in_sem.at[2]),
        pltpu.make_async_copy(cache_hbm, cache, in_sem.at[3]),
        pltpu.make_async_copy(qn_hbm, qn, in_sem.at[4]),
        pltpu.make_async_copy(qr_hbm, qr, in_sem.at[5]),
        pltpu.make_async_copy(own_hbm, own_ref, in_sem.at[6]),
        pltpu.make_async_copy(slot_hbm, slot_ref, in_sem.at[7]),
        pltpu.make_async_copy(len_hbm, len_ref, in_sem.at[8]),
    ]
    for load in loads[:2]:
        load.start()
    barrier = pltpu.get_barrier_semaphore()
    for who in partners:
        pl.semaphore_signal(barrier, inc=1, device_id=who, device_id_type=MESH)
    for load in loads[2:]:
        load.start()

    def rope_rows(rope, at, n):
        zero = jnp.zeros((64, n), BF16)
        ropes[0, :, pl.ds(at, n)] = jnp.concatenate([rope, zero], axis=0)
        ropes[1, :, pl.ds(at, n)] = jnp.concatenate([zero, rope], axis=0)

    def prefix_keys(i, _):
        at = pl.multiple_of(i * 256, 256)
        kv[:, pl.ds(at, 256)] = jnp.dot(
            up_t[...], cache[pl.ds(0, KVR), pl.ds(at, 256)], preferred_element_type=F32
        ).astype(BF16)
        rope_rows(cache[pl.ds(KVR, ROPE), pl.ds(at, 256)], at, 256)
        return _

    loads[0].wait()
    rows = nl[...]
    tiles = [rows[:, k * 128 : (k + 1) * 128] for k in range(4)]
    tiles.append(jnp.concatenate([rows[:, KVR:], jnp.zeros((16, 64), BF16)], axis=1))
    packed = jnp.concatenate(tiles, axis=0)
    ring[0, pl.ds(W_ROWS, NL_ROWS), :] = packed
    fresh[t] = packed
    loads[1].wait()
    pl.semaphore_wait(barrier, len(partners))

    def remote(src, dst, send, recv, who):
        return pltpu.make_async_remote_copy(
            src_ref=src, dst_ref=dst, send_sem=send, recv_sem=recv, device_id=who, device_id_type=MESH
        )

    def hop(b, k):
        at, n = PIECES[k]
        piece = pl.ds(at, n)
        return remote(ring.at[b, piece], ring.at[b + 2, piece], ring_send.at[0], ring_recv.at[b + 2, k], ring_to)

    coming = [(b, k) for b in range(2, 17) for k in range(len(PIECES))]

    def serve(n):
        for _ in range(n * len(PIECES) // 2):
            b, k = coming.pop(0)
            hop(b - 2, k).wait_recv()
            if b < 15:
                hop(b, k).start()

    first = remote(ring.at[0], ring.at[1], first_sem.at[0], first_sem.at[1], sibling)

    def new_rows(i):
        return remote(fresh.at[t], fresh.at[t], nl_sem.at[0], nl_sem.at[1], plane_peers[i])

    others = fresh.at[pl.ds(0, 15)]
    all_new_rows = remote(others, others, nl_sem.at[0], nl_sem.at[1], plane_peers[0])

    for k in range(len(PIECES)):
        hop(0, k).start()
    first.start()
    for i in range(15):
        new_rows(i).start()
    first.wait_recv()
    for k in range(len(PIECES)):
        hop(1, k).start()

    def look(n, codes):
        u, i = n // 2, lax.rem(n, 2)
        b = jnp.where(u > 0, u + 1, 0)
        plane = lax.rem(z - ahead * (b // 2) + Z, Z)
        block = 2 * (2 * plane + lax.rem(core + b, 2)) + i
        owner, place = own_ref[block], slot_ref[block]
        wanted = [(who, s) for who in (g, g + 1 - 2 * core) for s in range(SLOTS)]
        return tuple(
            jnp.where(jnp.logical_and(owner == who, place == s), 2 * b + i, old)
            for (who, s), old in zip(wanted, codes, strict=True)
        )


    for load in loads[2:4]:
        load.wait()
    up_t[...] = up[...].T
    lax.fori_loop(0, 2, prefix_keys, 0)
    lax.fori_loop(2, 5, prefix_keys, 0)
    serve(1)
    lax.fori_loop(5, 8, prefix_keys, 0)
    serve(2)
    all_new_rows.wait_recv()
    new = fresh[...].reshape(16, 5, 16, 128)
    new = [new[:, k].reshape(SPAN, 128) for k in range(5)]
    kv[:, pl.ds(PREFIX, SPAN)] = lax.dot_general(
        up_t[...], jnp.concatenate(new[:4], axis=1), (((1,), (1,)), ((), ())), preferred_element_type=F32
    ).astype(BF16)
    rope_rows(new[4].T[:ROPE], PREFIX, SPAN)

    for i in (4, 5, 8):
        loads[i].wait()
    to_bits = (NOPE + ROPE) ** -0.5 * 1.4426950408889634
    col = lax.broadcasted_iota(jnp.int32, (1, PREFIX), 1)
    old_bias = jnp.where(col < len_ref[0], 0.0, -1e30).astype(F32)
    row = lax.broadcasted_iota(jnp.int32, (SPAN, SPAN), 0)
    key = lax.broadcasted_iota(jnp.int32, (SPAN, SPAN), 1)
    token = ((key // 8) % 2) * 128 + (key // 16) * 8 + key % 8
    new_bias = jnp.where(token <= row, 0.0, -1e30).astype(F32)

    ones = jnp.ones((VDIM, KEYS), BF16)

    def weights(h):
        k = jnp.concatenate([kv[h * 256 : h * 256 + NOPE], ropes[h % 2]], axis=0)
        pair = h // 2
        q = jnp.concatenate([qn[:, h * 128 : (h + 1) * 128], qr[:, pair * 128 : (pair + 1) * 128]], axis=1)
        s = jnp.dot((q.astype(F32) * to_bits).astype(BF16), k, preferred_element_type=F32)
        s = jnp.concatenate([s[:, :PREFIX] + old_bias, s[:, PREFIX:] + new_bias], axis=1)
        return jnp.exp2(s - jnp.max(s, axis=1, keepdims=True)).astype(BF16)

    def attend(h, e):
        v = jnp.concatenate([kv[h * 256 + NOPE : (h + 1) * 256], ones], axis=0)
        o = lax.dot_general(e, v, (((1,), (1,)), ((), ())), preferred_element_type=F32)
        att[0, :, h * 128 : (h + 1) * 128] = (o[:, :VDIM] / o[:, VDIM:]).astype(BF16)

    def swap(h):
        cols = pl.ds(h * 128, 128)
        return remote(att.at[0, :, cols], att.at[1, :, cols], att_sem.at[0, h], att_sem.at[1, h], sibling)

    serve(2)
    e = weights(0)
    for h in range(1, HEADS_DEV):
        serve(1)
        attend(h - 1, e)
        e = weights(h)
        swap(h - 1).start()
        serve(1)
    attend(HEADS_DEV - 1, e)
    swap(HEADS_DEV - 1).start()
    serve(1)

    def part(s, *at):
        return part2.at[(s - 1, *at)] if s else part1.at[at]

    def mid(s, *at):
        return mid2.at[(s - 1, *at)] if s else mid1.at[at]

    def first_in(s, *at):
        return p1_2.at[(s - 1, *at)] if s else p1_1.at[at]

    def second_in(s, *at):
        return p2_2.at[(s - 1, *at)] if s else p2_1.at[at]

    def res(s):
        return res2.at[s - 1] if s else res1

    def res_in(s):
        return res_in2.at[s - 1] if s else res_in1

    def out_first(s, i):
        src = part(s, slice(None), slice(None), ys[i]) if s % 2 else part(s, slice(None), xs[i])
        who = y_peers[i] if s % 2 else x_peers[i]
        return remote(src, first_in(s, i), sums_send.at[int(s > 0)], p1_recv.at[s], who)

    def out_second(s, i):
        src = mid(s, slice(None), xs[i] if s % 2 else ys[i])
        who = x_peers[i] if s % 2 else y_peers[i]
        return remote(src, second_in(s, i), sums_send.at[2 + int(s > 0)], p2_recv.at[s], who)

    def out_res(s):
        return remote(res(s), res_in(s), sums_send.at[4 + int(s > 0)], res_recv.at[s], sibling)

    def out_far(f, i):
        xx, yy = plane_xy[i]
        return remote(part_far.at[f, :, xx, yy], direct.at[f, i], far_send.at[0, f], far_recv.at[0, f], plane_peers[i])

    def out_res_far(f):
        return remote(res_far.at[f], res_in_far.at[f], far_send.at[1, f], far_recv.at[1, f], sibling)

    def arrived(ref, sem):
        remote(ref, ref, sem, sem, sibling).wait_recv()

    def left(ref, sem):
        remote(ref, ref, sem, sem, sibling).wait_send()

    def times(blocks):
        w = [ring[b, pl.ds(0, W_ROWS), :] for b in blocks]
        a = att[...].reshape(2 * SPAN, W_ROWS)
        o = jnp.dot(a, jnp.concatenate(w, axis=1), preferred_element_type=F32).astype(BF16)
        return o.reshape(2, 4, 4, 16, 128 * len(w))

    def project(s):
        part(s)[...] = times((2 * s, 2 * s + 1) if s else (0,))
        for i in range(3):
            out_first(s, i).start()

    def project_far(f):
        part_far[f] = times((FAR[f],))
        for i in range(15):
            out_far(f, i).start()

    def add(own, terms):
        total = own[...].astype(F32)
        for term in terms:
            total += term[...].astype(F32)
        return total.astype(BF16)

    def first_sum(s):
        arrived(first_in(s), p1_recv.at[s])
        own = part(s, slice(None), slice(None), y) if s % 2 else part(s, slice(None), x)
        mid(s)[...] = add(own, [first_in(s, i) for i in range(3)])
        for i in range(3):
            out_second(s, i).start()

    def store(b, rows, core, ahead):
        plane = lax.rem(z - ahead * (b // 2) + Z, Z)
        for n in range(rows.shape[1] // 128):
            at = pl.multiple_of((2 * plane + lax.rem(core + b + n, 2)) * 128, 128)
            mixed_ref[:, pl.ds(at, 128)] = rows[:, n * 128 : (n + 1) * 128]

    def second_sum(s):
        arrived(second_in(s), p2_recv.at[s])
        own = mid(s, slice(None), x if s % 2 else y)
        total = add(own, [second_in(s, i) for i in range(3)])
        res(s)[...] = total[1]
        out_res(s).start()
        store(2 * s, total[0], core, ahead)

    def direct_sum(f):
        arrived(direct.at[f], far_recv.at[0, f])
        total = add(part_far.at[f, :, x, y], [direct.at[f, i] for i in range(15)])
        res_far[f] = total[1]
        out_res_far(f).start()
        store(FAR[f], total[0], core, ahead)

    def collect(s):
        arrived(res_in(s), res_recv.at[s])
        store(2 * s, res_in(s)[...], 1 - core, -ahead)

    def collect_far(f):
        arrived(res_in_far.at[f], far_recv.at[1, f])
        store(FAR[f], res_in_far[f], 1 - core, -ahead)

    for h in range(HEADS_DEV):
        swap(h).wait_recv()
    serve(1)
    project(0)
    project(1)
    serve(1)
    project(2)
    project(3)
    serve(2)
    project(4)
    for load in loads[6:8]:
        load.wait()
    codes = lax.fori_loop(0, 2 * Z, look, (jnp.int32(-1),) * (2 * SLOTS))
    serve(4)
    first_sum(0)
    project(5)
    serve(1)
    first_sum(1)
    serve(1)
    first_sum(2)
    serve(1)
    first_sum(3)
    serve(1)
    project(6)
    serve(1)
    first_sum(4)
    second_sum(0)
    serve(1)
    project_far(0)
    second_sum(1)
    first_sum(5)
    serve(2)
    project_far(1)
    first_sum(6)
    second_sum(2)
    serve(2)
    project_far(2)
    second_sum(3)
    second_sum(4)
    second_sum(5)
    assert not coming

    def pick(code):
        got = ring[jnp.maximum(code, 0) // 2, pl.ds(W_ROWS, NL_ROWS), :].reshape(5, 16, 128).astype(F32)
        got = jnp.where(lax.rem(jnp.maximum(code, 0), 2) == 0, got[:, :8], got[:, 8:])
        got = jnp.where(code >= 0, got, 0.0)
        return jnp.concatenate([got[k] for k in range(5)], axis=1)

    for s in range(0, SLOTS, 2):
        both = jnp.concatenate([pick(codes[SLOTS + s]), pick(codes[SLOTS + s + 1])], axis=0)
        dec[s // 2] = both.astype(BF16)
    swap_dec = remote(dec, dec_in, dec_sem.at[0], dec_sem.at[1], sibling)
    swap_dec.start()
    mine = [pick(codes[s]) for s in range(SLOTS)]
    swap_dec.wait_recv()
    for s in range(SLOTS):
        other = dec_in[s // 2].astype(F32)[(s % 2) * 8 : (s % 2) * 8 + 8]
        dec_ref[s] = (mine[s] + other)[:, :KVW].astype(BF16)

    for s in range(6):
        collect(s)
    direct_sum(0)
    direct_sum(1)
    second_sum(6)
    collect_far(0)
    collect_far(1)
    collect(6)
    left(ring.at[pl.ds(2, 15)], ring_send.at[0])
    first.wait_send()
    all_new_rows.wait_send()
    for h in range(HEADS_DEV):
        swap(h).wait_send()
    swap_dec.wait_send()
    for n, ref in enumerate((p1_1, p1_2, p2_1, p2_2, res_in1, res_in2)):
        left(ref, sums_send.at[n])
    for f in range(3):
        left(direct.at[f], far_send.at[0, f])
    direct_sum(2)
    collect_far(2)
    for f in range(3):
        left(res_in_far.at[f], far_send.at[1, f])


def body(query_nope, query_rope, latent_cache, new_latent, prefix_length, latent_up, out_proj, owners, slot_index):
    nl = new_latent.reshape(16, KVW)
    cache = latent_cache.T
    hbm = pl.BlockSpec(memory_space=pl.ANY)
    vmem = pl.BlockSpec(memory_space=pltpu.VMEM)
    dma = pltpu.SemaphoreType.DMA
    nk = len(PIECES)
    return pl.pallas_call(
        kernel,
        out_shape=(
            pltpu.VMEM((16, 4096), BF16),
            pltpu.VMEM((SLOTS, 8, KVW), BF16),
        ),
        in_specs=[hbm] * 9,
        out_specs=(vmem, vmem),
        scratch_shapes=[
            pltpu.SMEM((1,), jnp.int32),
            pltpu.SMEM((64,), jnp.int32),
            pltpu.SMEM((64,), jnp.int32),
            pltpu.VMEM((SPAN, 512), BF16),
            pltpu.VMEM((SPAN, 256), BF16),
            pltpu.VMEM((KVW, PREFIX), BF16),
            pltpu.VMEM((KVR, 1024), BF16),
            pltpu.VMEM((16, KVW), BF16),
            pltpu.VMEM((16, NL_ROWS, 128), BF16),
            pltpu.VMEM((1024, KVR), BF16),
            pltpu.VMEM((1024, KEYS), BF16),
            pltpu.VMEM((2, 128, KEYS), BF16),
            pltpu.VMEM((17, BLK_ROWS, 128), BF16),
            pltpu.VMEM((2, SPAN, 512), BF16),
            pltpu.VMEM((2, 4, 4, 16, 128), BF16),
            pltpu.VMEM((6, 2, 4, 4, 16, 256), BF16),
            pltpu.VMEM((3, 2, 4, 16, 128), BF16),
            pltpu.VMEM((6, 3, 2, 4, 16, 256), BF16),
            pltpu.VMEM((2, 4, 16, 128), BF16),
            pltpu.VMEM((6, 2, 4, 16, 256), BF16),
            pltpu.VMEM((3, 2, 16, 128), BF16),
            pltpu.VMEM((6, 3, 2, 16, 256), BF16),
            pltpu.VMEM((16, 128), BF16),
            pltpu.VMEM((6, 16, 256), BF16),
            pltpu.VMEM((16, 128), BF16),
            pltpu.VMEM((6, 16, 256), BF16),
            pltpu.VMEM((3, 2, 4, 4, 16, 128), BF16),
            pltpu.VMEM((3, 15, 2, 16, 128), BF16),
            pltpu.VMEM((3, 16, 128), BF16),
            pltpu.VMEM((3, 16, 128), BF16),
            pltpu.VMEM((2, 16, 640), BF16),
            pltpu.VMEM((2, 16, 640), BF16),
            dma((9,)),
            dma((1,)),
            dma((17, nk)),
            dma((2,)),
            dma((2,)),
            dma((2, HEADS_DEV)),
            dma((6,)),
            dma((7,)),
            dma((7,)),
            dma((7,)),
            dma((2, 3)),
            dma((2, 3)),
            dma((2,)),
        ],
        compiler_params=pltpu.CompilerParams(
            collective_id=0, has_side_effects=True, vmem_limit_bytes=56 * 1024 * 1024
        ),
        cost_estimate=pl.CostEstimate(flops=5_000_000_000, bytes_accessed=6_000_000, transcendentals=2_400_000),
    )(prefix_length, owners, slot_index, query_nope, query_rope, cache, nl, latent_up, out_proj)


def solution(mesh):
    placed = (
        P("grp", "tp"),
        P("grp", "tp"),
        P("grp", None),
        P("grp", "tp", None),
        P("grp"),
        P(None, "tp"),
        P("tp", "grp"),
        P(),
        P(),
    )
    return jax.shard_map(
        body,
        mesh=mesh,
        in_specs=placed,
        out_specs=(P(("grp", "tp"), None), P("grp", "tp", None)),
        check_vma=False,
    )
```

```python
import jax
import jax.numpy as jnp
from jax import lax
from jax.experimental import pallas as pl
from jax.experimental.pallas import tpu as pltpu
from jax.sharding import PartitionSpec as P

NOPE = 128
ROPE = 64
VDIM = 128
KVR = 512
KVW = 576
SLOTS = 4
SPAN = 256
PREFIX = 2048
KEYS = PREFIX + SPAN
HEADS_DEV = 4
GRP = 32
Z = 16
W_ROWS = 512
NL_ROWS = 80
BLK_ROWS = W_ROWS + NL_ROWS
PIECES = ((0, 304), (304, 288))
NEAR = range(7)
FAR = (14, 15, 16)
MESH = pl.DeviceIdType.MESH
F32 = jnp.float32
BF16 = jnp.bfloat16


def kernel(
    len_hbm, own_hbm, slot_hbm, qn_hbm, qr_hbm, cache_hbm, nl_hbm, up_hbm, w_hbm,
    mixed_ref, dec_ref,
    len_ref, own_ref, slot_ref, qn, qr, cache, up, nl, fresh, up_t, kv, ropes, ring, att, part1, part2, p1_1, p1_2, mid1, mid2, p2_1, p2_2,
    res1, res2, res_in1, res_in2, part_far, direct, res_far, res_in_far, dec, dec_in,
    in_sem, ring_send, ring_recv, first_sem, nl_sem, att_sem, sums_send, p1_recv, p2_recv, res_recv, far_send, far_recv,
    dec_sem,
):
    g = lax.axis_index("grp")
    t = lax.axis_index("tp")
    z, core = g // 2, lax.rem(g, 2)
    x, y = t // 4, lax.rem(t, 4)
    ahead = 1 - 2 * core
    ring_to = {"grp": lax.rem(g + 2 * ahead + GRP, GRP)}
    ring_from = {"grp": lax.rem(g - 2 * ahead + GRP, GRP)}
    sibling = {"grp": g + 1 - 2 * core}
    xs = [lax.rem(x + d, 4) for d in (2, 1, 3)]
    ys = [lax.rem(y + d, 4) for d in (2, 1, 3)]
    x_peers = [{"tp": xx * 4 + y} for xx in xs]
    y_peers = [{"tp": x * 4 + yy} for yy in ys]

    plane = [(dx, dy) for dx in range(4) for dy in range(4)][1:]
    plane.sort(key=lambda d: -min(d[0], 4 - d[0]) - min(d[1], 4 - d[1]))
    plane_xy = [(lax.rem(x + dx, 4), lax.rem(y + dy, 4)) for dx, dy in plane]
    plane_peers = [{"tp": xx * 4 + yy} for xx, yy in plane_xy]
    partners = plane_peers + [ring_from, ring_to, sibling]

    loads = [
        pltpu.make_async_copy(nl_hbm, nl, in_sem.at[0]),
        pltpu.make_async_copy(w_hbm, ring.at[0, pl.ds(0, W_ROWS)], in_sem.at[1]),
        pltpu.make_async_copy(up_hbm, up, in_sem.at[2]),
        pltpu.make_async_copy(cache_hbm, cache, in_sem.at[3]),
        pltpu.make_async_copy(qn_hbm, qn, in_sem.at[4]),
        pltpu.make_async_copy(qr_hbm, qr, in_sem.at[5]),
        pltpu.make_async_copy(own_hbm, own_ref, in_sem.at[6]),
        pltpu.make_async_copy(slot_hbm, slot_ref, in_sem.at[7]),
        pltpu.make_async_copy(len_hbm, len_ref, in_sem.at[8]),
    ]
    for load in loads[:2]:
        load.start()
    barrier = pltpu.get_barrier_semaphore()
    for who in partners:
        pl.semaphore_signal(barrier, inc=1, device_id=who, device_id_type=MESH)
    for load in loads[2:]:
        load.start()

    def rope_rows(rope, at, n):
        zero = jnp.zeros((64, n), BF16)
        ropes[0, :, pl.ds(at, n)] = jnp.concatenate([rope, zero], axis=0)
        ropes[1, :, pl.ds(at, n)] = jnp.concatenate([zero, rope], axis=0)

    def prefix_keys(i, _):
        at = pl.multiple_of(i * 256, 256)
        kv[:, pl.ds(at, 256)] = jnp.dot(
            up_t[...], cache[pl.ds(0, KVR), pl.ds(at, 256)], preferred_element_type=F32
        ).astype(BF16)
        rope_rows(cache[pl.ds(KVR, ROPE), pl.ds(at, 256)], at, 256)
        return _

    loads[0].wait()
    rows = nl[...]
    tiles = [rows[:, k * 128 : (k + 1) * 128] for k in range(4)]
    tiles.append(jnp.concatenate([rows[:, KVR:], jnp.zeros((16, 64), BF16)], axis=1))
    packed = jnp.concatenate(tiles, axis=0)
    ring[0, pl.ds(W_ROWS, NL_ROWS), :] = packed
    fresh[t] = packed
    loads[1].wait()
    pl.semaphore_wait(barrier, len(partners))

    def remote(src, dst, send, recv, who):
        return pltpu.make_async_remote_copy(
            src_ref=src, dst_ref=dst, send_sem=send, recv_sem=recv, device_id=who, device_id_type=MESH
        )

    def hop(b, k):
        at, n = PIECES[k]
        piece = pl.ds(at, n)
        return remote(ring.at[b, piece], ring.at[b + 2, piece], ring_send.at[0], ring_recv.at[b + 2, k], ring_to)

    coming = [(b, k) for b in range(2, 17) for k in range(len(PIECES))]

    def serve(n):
        for _ in range(n * len(PIECES) // 2):
            b, k = coming.pop(0)
            hop(b - 2, k).wait_recv()
            if b < 15:
                hop(b, k).start()

    first = remote(ring.at[0], ring.at[1], first_sem.at[0], first_sem.at[1], sibling)

    def new_rows(i):
        return remote(fresh.at[t], fresh.at[t], nl_sem.at[0], nl_sem.at[1], plane_peers[i])

    others = fresh.at[pl.ds(0, 15)]
    all_new_rows = remote(others, others, nl_sem.at[0], nl_sem.at[1], plane_peers[0])

    for k in range(len(PIECES)):
        hop(0, k).start()
    first.start()
    for i in range(15):
        new_rows(i).start()
    first.wait_recv()
    for k in range(len(PIECES)):
        hop(1, k).start()

    def look(n, codes):
        u, i = n // 2, lax.rem(n, 2)
        b = jnp.where(u > 0, u + 1, 0)
        plane = lax.rem(z - ahead * (b // 2) + Z, Z)
        block = 2 * (2 * plane + lax.rem(core + b, 2)) + i
        owner, place = own_ref[block], slot_ref[block]
        wanted = [(who, s) for who in (g, g + 1 - 2 * core) for s in range(SLOTS)]
        return tuple(
            jnp.where(jnp.logical_and(owner == who, place == s), 2 * b + i, old)
            for (who, s), old in zip(wanted, codes, strict=True)
        )


    for load in loads[2:4]:
        load.wait()
    up_t[...] = up[...].T
    lax.fori_loop(0, 2, prefix_keys, 0)
    lax.fori_loop(2, 5, prefix_keys, 0)
    serve(1)
    lax.fori_loop(5, 8, prefix_keys, 0)
    serve(2)
    all_new_rows.wait_recv()
    new = fresh[...].reshape(16, 5, 16, 128)
    new = [new[:, k].reshape(SPAN, 128) for k in range(5)]
    kv[:, pl.ds(PREFIX, SPAN)] = lax.dot_general(
        up_t[...], jnp.concatenate(new[:4], axis=1), (((1,), (1,)), ((), ())), preferred_element_type=F32
    ).astype(BF16)
    rope_rows(new[4].T[:ROPE], PREFIX, SPAN)

    for i in (4, 5, 8):
        loads[i].wait()
    to_bits = (NOPE + ROPE) ** -0.5 * 1.4426950408889634
    col = lax.broadcasted_iota(jnp.int32, (1, PREFIX), 1)
    old_bias = jnp.where(col < len_ref[0], 0.0, -1e30).astype(F32)
    row = lax.broadcasted_iota(jnp.int32, (SPAN, SPAN), 0)
    key = lax.broadcasted_iota(jnp.int32, (SPAN, SPAN), 1)
    token = ((key // 8) % 2) * 128 + (key // 16) * 8 + key % 8
    new_bias = jnp.where(token <= row, 0.0, -1e30).astype(F32)

    ones = jnp.ones((VDIM, KEYS), BF16)

    def weights(h):
        k = jnp.concatenate([kv[h * 256 : h * 256 + NOPE], ropes[h % 2]], axis=0)
        pair = h // 2
        q = jnp.concatenate([qn[:, h * 128 : (h + 1) * 128], qr[:, pair * 128 : (pair + 1) * 128]], axis=1)
        s = jnp.dot(q, k, preferred_element_type=F32)
        s = jnp.concatenate([s[:, :PREFIX] + old_bias, s[:, PREFIX:] + new_bias], axis=1)
        return jnp.exp2((s - jnp.max(s, axis=1, keepdims=True)) * to_bits).astype(BF16)

    def attend(h, e):
        v = jnp.concatenate([kv[h * 256 + NOPE : (h + 1) * 256], ones], axis=0)
        o = lax.dot_general(e, v, (((1,), (1,)), ((), ())), preferred_element_type=F32)
        att[0, :, h * 128 : (h + 1) * 128] = (o[:, :VDIM] / o[:, VDIM:]).astype(BF16)

    def swap(h):
        cols = pl.ds(h * 128, 128)
        return remote(att.at[0, :, cols], att.at[1, :, cols], att_sem.at[0, h], att_sem.at[1, h], sibling)

    serve(2)
    e = weights(0)
    for h in range(1, HEADS_DEV):
        serve(1)
        attend(h - 1, e)
        e = weights(h)
        swap(h - 1).start()
        serve(1)
    attend(HEADS_DEV - 1, e)
    swap(HEADS_DEV - 1).start()
    serve(1)

    def part(s, *at):
        return part2.at[(s - 1, *at)] if s else part1.at[at]

    def mid(s, *at):
        return mid2.at[(s - 1, *at)] if s else mid1.at[at]

    def first_in(s, *at):
        return p1_2.at[(s - 1, *at)] if s else p1_1.at[at]

    def second_in(s, *at):
        return p2_2.at[(s - 1, *at)] if s else p2_1.at[at]

    def res(s):
        return res2.at[s - 1] if s else res1

    def res_in(s):
        return res_in2.at[s - 1] if s else res_in1

    def out_first(s, i):
        src = part(s, slice(None), slice(None), ys[i]) if s % 2 else part(s, slice(None), xs[i])
        who = y_peers[i] if s % 2 else x_peers[i]
        return remote(src, first_in(s, i), sums_send.at[int(s > 0)], p1_recv.at[s], who)

    def out_second(s, i):
        src = mid(s, slice(None), xs[i] if s % 2 else ys[i])
        who = x_peers[i] if s % 2 else y_peers[i]
        return remote(src, second_in(s, i), sums_send.at[2 + int(s > 0)], p2_recv.at[s], who)

    def out_res(s):
        return remote(res(s), res_in(s), sums_send.at[4 + int(s > 0)], res_recv.at[s], sibling)

    def out_far(f, i):
        xx, yy = plane_xy[i]
        return remote(part_far.at[f, :, xx, yy], direct.at[f, i], far_send.at[0, f], far_recv.at[0, f], plane_peers[i])

    def out_res_far(f):
        return remote(res_far.at[f], res_in_far.at[f], far_send.at[1, f], far_recv.at[1, f], sibling)

    def arrived(ref, sem):
        remote(ref, ref, sem, sem, sibling).wait_recv()

    def left(ref, sem):
        remote(ref, ref, sem, sem, sibling).wait_send()

    def times(blocks):
        w = [ring[b, pl.ds(0, W_ROWS), :] for b in blocks]
        a = att[...].reshape(2 * SPAN, W_ROWS)
        o = jnp.dot(a, jnp.concatenate(w, axis=1), preferred_element_type=F32).astype(BF16)
        return o.reshape(2, 4, 4, 16, 128 * len(w))

    def project(s):
        part(s)[...] = times((2 * s, 2 * s + 1) if s else (0,))
        for i in range(3):
            out_first(s, i).start()

    def project_far(f):
        part_far[f] = times((FAR[f],))
        for i in range(15):
            out_far(f, i).start()

    def add(own, terms):
        total = own[...].astype(F32)
        for term in terms:
            total += term[...].astype(F32)
        return total.astype(BF16)

    def first_sum(s):
        arrived(first_in(s), p1_recv.at[s])
        own = part(s, slice(None), slice(None), y) if s % 2 else part(s, slice(None), x)
        mid(s)[...] = add(own, [first_in(s, i) for i in range(3)])
        for i in range(3):
            out_second(s, i).start()

    def store(b, rows, core, ahead):
        plane = lax.rem(z - ahead * (b // 2) + Z, Z)
        for n in range(rows.shape[1] // 128):
            at = pl.multiple_of((2 * plane + lax.rem(core + b + n, 2)) * 128, 128)
            mixed_ref[:, pl.ds(at, 128)] = rows[:, n * 128 : (n + 1) * 128]

    def second_sum(s):
        arrived(second_in(s), p2_recv.at[s])
        own = mid(s, slice(None), x if s % 2 else y)
        total = add(own, [second_in(s, i) for i in range(3)])
        res(s)[...] = total[1]
        out_res(s).start()
        store(2 * s, total[0], core, ahead)

    def direct_sum(f):
        arrived(direct.at[f], far_recv.at[0, f])
        total = add(part_far.at[f, :, x, y], [direct.at[f, i] for i in range(15)])
        res_far[f] = total[1]
        out_res_far(f).start()
        store(FAR[f], total[0], core, ahead)

    def collect(s):
        arrived(res_in(s), res_recv.at[s])
        store(2 * s, res_in(s)[...], 1 - core, -ahead)

    def collect_far(f):
        arrived(res_in_far.at[f], far_recv.at[1, f])
        store(FAR[f], res_in_far[f], 1 - core, -ahead)

    for h in range(HEADS_DEV):
        swap(h).wait_recv()
    serve(1)
    project(0)
    project(1)
    serve(1)
    project(2)
    project(3)
    serve(2)
    project(4)
    for load in loads[6:8]:
        load.wait()
    codes = lax.fori_loop(0, 2 * Z, look, (jnp.int32(-1),) * (2 * SLOTS))
    serve(4)
    first_sum(0)
    project(5)
    serve(1)
    first_sum(1)
    serve(1)
    first_sum(2)
    serve(1)
    first_sum(3)
    serve(1)
    project(6)
    serve(1)
    first_sum(4)
    second_sum(0)
    serve(1)
    project_far(0)
    second_sum(1)
    first_sum(5)
    serve(2)
    project_far(1)
    first_sum(6)
    second_sum(2)
    serve(2)
    project_far(2)
    second_sum(3)
    second_sum(4)
    second_sum(5)
    assert not coming

    def pick(code):
        got = ring[jnp.maximum(code, 0) // 2, pl.ds(W_ROWS, NL_ROWS), :].reshape(5, 16, 128).astype(F32)
        got = jnp.where(lax.rem(jnp.maximum(code, 0), 2) == 0, got[:, :8], got[:, 8:])
        got = jnp.where(code >= 0, got, 0.0)
        return jnp.concatenate([got[k] for k in range(5)], axis=1)

    for s in range(0, SLOTS, 2):
        both = jnp.concatenate([pick(codes[SLOTS + s]), pick(codes[SLOTS + s + 1])], axis=0)
        dec[s // 2] = both.astype(BF16)
    swap_dec = remote(dec, dec_in, dec_sem.at[0], dec_sem.at[1], sibling)
    swap_dec.start()
    mine = [pick(codes[s]) for s in range(SLOTS)]
    for s in range(6):
        collect(s)
    direct_sum(0)
    direct_sum(1)
    second_sum(6)
    swap_dec.wait_recv()
    for s in range(SLOTS):
        other = dec_in[s // 2].astype(F32)[(s % 2) * 8 : (s % 2) * 8 + 8]
        dec_ref[s] = (mine[s] + other)[:, :KVW].astype(BF16)
    collect_far(0)
    collect_far(1)
    collect(6)
    left(ring.at[pl.ds(2, 15)], ring_send.at[0])
    first.wait_send()
    all_new_rows.wait_send()
    for h in range(HEADS_DEV):
        swap(h).wait_send()
    swap_dec.wait_send()
    for n, ref in enumerate((p1_1, p1_2, p2_1, p2_2, res_in1, res_in2)):
        left(ref, sums_send.at[n])
    for f in range(3):
        left(direct.at[f], far_send.at[0, f])
    direct_sum(2)
    collect_far(2)
    for f in range(3):
        left(res_in_far.at[f], far_send.at[1, f])


def body(query_nope, query_rope, latent_cache, new_latent, prefix_length, latent_up, out_proj, owners, slot_index):
    nl = new_latent.reshape(16, KVW)
    cache = latent_cache.T
    hbm = pl.BlockSpec(memory_space=pl.ANY)
    vmem = pl.BlockSpec(memory_space=pltpu.VMEM)
    dma = pltpu.SemaphoreType.DMA
    nk = len(PIECES)
    return pl.pallas_call(
        kernel,
        out_shape=(
            pltpu.VMEM((16, 4096), BF16),
            pltpu.VMEM((SLOTS, 8, KVW), BF16),
        ),
        in_specs=[hbm] * 9,
        out_specs=(vmem, vmem),
        scratch_shapes=[
            pltpu.SMEM((1,), jnp.int32),
            pltpu.SMEM((64,), jnp.int32),
            pltpu.SMEM((64,), jnp.int32),
            pltpu.VMEM((SPAN, 512), BF16),
            pltpu.VMEM((SPAN, 256), BF16),
            pltpu.VMEM((KVW, PREFIX), BF16),
            pltpu.VMEM((KVR, 1024), BF16),
            pltpu.VMEM((16, KVW), BF16),
            pltpu.VMEM((16, NL_ROWS, 128), BF16),
            pltpu.VMEM((1024, KVR), BF16),
            pltpu.VMEM((1024, KEYS), BF16),
            pltpu.VMEM((2, 128, KEYS), BF16),
            pltpu.VMEM((17, BLK_ROWS, 128), BF16),
            pltpu.VMEM((2, SPAN, 512), BF16),
            pltpu.VMEM((2, 4, 4, 16, 128), BF16),
            pltpu.VMEM((6, 2, 4, 4, 16, 256), BF16),
            pltpu.VMEM((3, 2, 4, 16, 128), BF16),
            pltpu.VMEM((6, 3, 2, 4, 16, 256), BF16),
            pltpu.VMEM((2, 4, 16, 128), BF16),
            pltpu.VMEM((6, 2, 4, 16, 256), BF16),
            pltpu.VMEM((3, 2, 16, 128), BF16),
            pltpu.VMEM((6, 3, 2, 16, 256), BF16),
            pltpu.VMEM((16, 128), BF16),
            pltpu.VMEM((6, 16, 256), BF16),
            pltpu.VMEM((16, 128), BF16),
            pltpu.VMEM((6, 16, 256), BF16),
            pltpu.VMEM((3, 2, 4, 4, 16, 128), BF16),
            pltpu.VMEM((3, 15, 2, 16, 128), BF16),
            pltpu.VMEM((3, 16, 128), BF16),
            pltpu.VMEM((3, 16, 128), BF16),
            pltpu.VMEM((2, 16, 640), BF16),
            pltpu.VMEM((2, 16, 640), BF16),
            dma((9,)),
            dma((1,)),
            dma((17, nk)),
            dma((2,)),
            dma((2,)),
            dma((2, HEADS_DEV)),
            dma((6,)),
            dma((7,)),
            dma((7,)),
            dma((7,)),
            dma((2, 3)),
            dma((2, 3)),
            dma((2,)),
        ],
        compiler_params=pltpu.CompilerParams(
            collective_id=0, has_side_effects=True, vmem_limit_bytes=56 * 1024 * 1024
        ),
        cost_estimate=pl.CostEstimate(flops=5_000_000_000, bytes_accessed=6_000_000, transcendentals=2_400_000),
    )(prefix_length, owners, slot_index, query_nope, query_rope, cache, nl, latent_up, out_proj)


def solution(mesh):
    placed = (
        P("grp", "tp"),
        P("grp", "tp"),
        P("grp", None),
        P("grp", "tp", None),
        P("grp"),
        P(None, "tp"),
        P("tp", "grp"),
        P(),
        P(),
    )
    return jax.shard_map(
        body,
        mesh=mesh,
        in_specs=placed,
        out_specs=(P(("grp", "tp"), None), P("grp", "tp", None)),
        check_vma=False,
    )
```
